256 devices in a mesh: dp: 64 (over x, z, core), clus: 4 (over y).
Axes of the slice: x: 4, y: 4, z: 8, core: 2. Of those that a mesh axis runs over, the one named last changes fastest.
Arguments:
- embeds: float32 [32768, 1024], P(('dp', 'clus')), may hold values from -300 to 300
- cluster_ids: int32 [32768], P(('dp', 'clus')), may hold values from 0 to 255, as said below
- inv_temp: float32 [256], P('dp'), may hold values from 40 to 400
Outputs:
- residual: float32 [32768, 1024], P(('dp', 'clus'))
- similarity: float32 [32768], P(('dp', 'clus'))
The draws below stay inside these ranges and needn't reach their ends.
Inputs may be any that keep to these rules, and one draw needn't show every extreme that they name: `cluster_ids`: cluster c belongs to owner c // 4. Rows lie in aligned blocks of 128 rows, one block a device, in the order dp, clus. In every block at most 8 rows belong to clusters of one owner, and exactly 8 belong to one owner that is the same for all blocks of one index of clus. Every row shares its cluster with at least one other row of its block.
All inputs are finite; a program needn't handle non-finite values.
Results may differ from the reference program's by a relative error of at most 0.011.
Values may be sent and summed in bfloat16 or wider, within the bound.
A program may use at most 64 MiB of HBM per device.

```python
import math
import jax
import jax.numpy as jnp
from jax import lax

D = 1024
ROW_DEV = 128
CL_DEV = 4
CAP = 8
ROWS = 32768
CLUSTERS = 256
N_DP = 64
N_CLUS = 4
DEVICES = 256


def cluster_plan(key):
    pair_count = ROW_DEV // 2
    half_cap = CAP // 2
    hot_owner = jax.random.randint(jax.random.fold_in(key, 11), (N_CLUS,), 0, N_DP)

    def one_block(block_index):
        block_key = jax.random.fold_in(key, 1000 + block_index)
        column = block_index % N_CLUS
        hottest = hot_owner[column]
        others = jax.random.permutation(jax.random.fold_in(block_key, 1), (N_DP - 1) * half_cap)
        others = jnp.where(others >= hottest * half_cap, others + half_cap, others)
        hot_slots = hottest * half_cap + jnp.arange(half_cap)
        pair_slots = jnp.concatenate([hot_slots, others])[:pair_count]
        owner_of = pair_slots // half_cap
        sub_cluster = jax.random.randint(jax.random.fold_in(block_key, 2), (pair_count,), 0, CL_DEV)
        pair_cluster = owner_of * CL_DEV + sub_cluster
        shuffled = jax.random.permutation(jax.random.fold_in(block_key, 3), ROW_DEV)
        return pair_cluster[shuffled // 2]
    return jax.vmap(one_block)(jnp.arange(DEVICES)).reshape(-1).astype(jnp.int32)


def draw_cluster_ids(key, part):
    return cluster_plan(key)


def draw_embeds(key, part):
    cluster_of = cluster_plan(key)
    key = jax.random.fold_in(key, 5)
    base_rows = jax.random.truncated_normal(jax.random.fold_in(key, 1), -4.0, 4.0, (CLUSTERS, D), jnp.float32)
    noise_rows = jax.random.truncated_normal(jax.random.fold_in(key, 2), -4.0, 4.0, (ROWS, D), jnp.float32)
    strength = jax.random.uniform(jax.random.fold_in(key, 3), (CLUSTERS,), jnp.float32, 0.3, 1.0)
    row_scale = jnp.exp(jax.random.uniform(jax.random.fold_in(key, 4), (ROWS,), jnp.float32, 0.0, math.log(10.0)))
    mixed = strength[cluster_of][:, None] * base_rows[cluster_of] + noise_rows
    return (row_scale[:, None] * mixed).astype(jnp.float32)


def draw_inv_temp(key, part):
    key = jax.random.fold_in(key, 7)
    return jnp.exp(jax.random.uniform(jax.random.fold_in(key, 1), (CLUSTERS,), jnp.float32, math.log(40.0), math.log(400.0))).astype(jnp.float32)


def setup_inputs(seed: int = 0) -> dict:
    key_of = jax.random.split(jax.random.key(seed), 4)
    return {
        "embeds": draw_embeds(jax.random.fold_in(key_of[3], 71), 0),
        "cluster_ids": draw_cluster_ids(jax.random.fold_in(key_of[3], 71), 0),
        "inv_temp": draw_inv_temp(jax.random.fold_in(key_of[3], 71), 0),
    }


lowest_score = -1e+30

def reference(embeds, cluster_ids, inv_temp):
    total_rows = embeds.shape[0]
    unit_rows = embeds * lax.rsqrt(lax.optimization_barrier(jnp.sum(embeds * embeds, axis=1, keepdims=True)) + 1e-06)
    packed = lax.optimization_barrier(unit_rows.astype(jnp.bfloat16)).astype(jnp.float32)
    owner_of = (cluster_ids // CL_DEV).astype(jnp.int32)
    group_rows = DEVICES * CAP
    query_block = min(256, group_rows)
    ordering = jnp.argsort(owner_of, stable=True).astype(jnp.int32)
    owner_counts = lax.optimization_barrier(jnp.sum((owner_of[:, None] == jnp.arange(N_DP, dtype=jnp.int32)[None, :]).astype(jnp.int32), axis=0)).astype(jnp.int32)
    owner_starts = (jnp.cumsum(owner_counts) - owner_counts).astype(jnp.int32)
    row_temp = inv_temp[cluster_ids]
    sorted_rows = jnp.concatenate([packed[ordering], jnp.zeros((group_rows, D), packed.dtype)], axis=0)
    sorted_ids = jnp.concatenate([cluster_ids[ordering], jnp.full((group_rows,), -1, jnp.int32)])
    sorted_index = jnp.concatenate([ordering, jnp.full((group_rows,), total_rows, jnp.int32)])
    sorted_temp = jnp.concatenate([row_temp[ordering], jnp.ones((group_rows,), row_temp.dtype)])

    def per_owner(running, owner):
        near_all, close_all = running
        begin = owner_starts[owner].astype(jnp.int32)
        member_count = owner_counts[owner]
        key_rows = lax.dynamic_slice_in_dim(sorted_rows, begin, group_rows, 0)
        valid = jnp.arange(group_rows, dtype=jnp.int32) < member_count
        key_ids = jnp.where(valid, lax.dynamic_slice_in_dim(sorted_ids, begin, group_rows, 0), -1)
        key_index = jnp.where(valid, lax.dynamic_slice_in_dim(sorted_index, begin, group_rows, 0), total_rows)
        key_temp = lax.dynamic_slice_in_dim(sorted_temp, begin, group_rows, 0)

        def one_block(block_index):
            first_row = (block_index * query_block).astype(jnp.int32)

            def compute(unused):
                queries = lax.dynamic_slice_in_dim(key_rows, first_row, query_block, 0)
                query_ids = lax.dynamic_slice_in_dim(key_ids, first_row, query_block, 0)
                query_index = lax.dynamic_slice_in_dim(key_index, first_row, query_block, 0)
                query_temp = lax.dynamic_slice_in_dim(key_temp, first_row, query_block, 0)
                cosine = jnp.dot(queries, key_rows.T, precision=lax.Precision.HIGHEST)
                scores = query_temp[:, None] * cosine
                allowed = (query_ids[:, None] == key_ids[None, :]) & (query_ids[:, None] >= 0) & (query_index[:, None] != key_index[None, :])
                top_score = lax.optimization_barrier(jnp.max(jnp.where(allowed, scores, lowest_score), axis=1))
                weights = jnp.where(allowed, jnp.exp(scores - top_score[:, None]), 0.0)
                weight_total = lax.optimization_barrier(jnp.sum(weights, axis=1))
                rounded = lax.optimization_barrier(weights.astype(jnp.bfloat16)).astype(jnp.float32)
                summed = jnp.dot(rounded, key_rows, precision=lax.Precision.HIGHEST)
                near = summed / jnp.where(weight_total > 0, weight_total, 1.0)[:, None]
                close = jnp.where(query_ids >= 0, top_score / query_temp, 0.0)
                return (near, close)

            def skipped(unused):
                return (jnp.zeros((query_block, D), packed.dtype), jnp.zeros((query_block,), packed.dtype))
            return lax.cond(first_row < member_count, compute, skipped, 0)
        near, close = lax.map(one_block, jnp.arange(group_rows // query_block, dtype=jnp.int32))
        near = near.reshape(group_rows, D)
        close = close.reshape(group_rows)
        near_all = near_all.at[key_index].set(near, mode='drop')
        close_all = close_all.at[key_index].set(close, mode='drop')
        return ((near_all, close_all), None)
    initial = (jnp.zeros((total_rows, D), packed.dtype), jnp.zeros((total_rows,), packed.dtype))
    (near_all, close_all), unused = lax.scan(per_owner, initial, jnp.arange(N_DP, dtype=jnp.int32))
    return (unit_rows - near_all, close_all)
```

```python
import functools

import jax
import jax.numpy as jnp
from jax import lax
from jax.experimental import pallas as pl
from jax.experimental.pallas import tpu as pltpu
from jax.sharding import PartitionSpec as P

NX, NZ, NC, NY = 4, 8, 2, 4
CAP = 8
LOWEST = -1e30
MESH = pl.DeviceIdType.MESH
F32 = jnp.float32
BF16 = jnp.bfloat16


def wait_bytes(ref, sem):
    pltpu.make_async_copy(ref, ref, sem).wait()


def kernel(
    ids_ref, x_ref, temp_ref, out_ref, sim_ref,
    unit, halves, send, keys, table, scores, weights, outs, back, turned,
    id_send, id_recv, key_ids, sim_send, sim_recv,
    row_send_sem, row_recv_sem, right_send_sem, left_send_sem, relay_send_sem,
    y_recv_sem, far_recv_sem, id_send_sem, id_recv_sem, kid_send_sem, kid_recv_sem,
    back_send_sem, back_recv_sem, sim_send_sem, sim_recv_sem,
):
    group = NX * NC
    owners = group * NZ
    rows, width = x_ref.shape
    half = width // 2
    slots = owners * CAP
    per_owner = temp_ref.shape[0]
    chunk_rows = group * CAP

    me = lax.axis_index("dp")
    my_y = lax.axis_index("clus")
    my_c = lax.rem(me, NC)
    my_z = lax.rem(lax.div(me, NC), NZ)
    my_x = lax.div(me, NC * NZ)
    y_right = lax.rem(my_y + 1, NY)
    y_left = lax.rem(my_y + NY - 1, NY)
    y_far = lax.rem(my_y + 2, NY)

    def shift_of(k):
        m = lax.div(k, group)
        g = lax.rem(k, group)
        odd = lax.rem(m, 2)
        dz = odd * lax.div(m + 1, 2) + (1 - odd) * lax.rem(NZ - lax.div(m, 2), NZ)
        return lax.div(g, NC), dz, lax.rem(g, NC)

    def ahead(k):
        dx, dz, dc = shift_of(k)
        x, z, c = lax.rem(my_x + dx, NX), lax.rem(my_z + dz, NZ), lax.rem(my_c + dc, NC)
        return (x * NZ + z) * NC + c

    def behind(k):
        dx, dz, dc = shift_of(k)
        x, z, c = lax.rem(my_x + NX - dx, NX), lax.rem(my_z + NZ - dz, NZ), lax.rem(my_c + NC - dc, NC)
        return (x * NZ + z) * NC + c

    barrier = pltpu.get_barrier_semaphore()

    @pl.loop(1, owners)
    def _(k):
        pl.semaphore_signal(barrier, inc=1, device_id=(ahead(k), my_y), device_id_type=MESH)

    for y in (y_right, y_left, y_far):
        pl.semaphore_signal(barrier, inc=1, device_id=(me, y), device_id_type=MESH)

    x = x_ref[...]
    unit_rows = x * lax.rsqrt(jnp.sum(x * x, axis=1, keepdims=True) + 1e-06)
    unit[...] = unit_rows
    packed = unit_rows.astype(BF16)
    halves[:rows, :] = packed[:, :half]
    halves[rows:, :] = packed[:, half:]

    ids = ids_ref[...]
    owner = lax.div(ids, per_owner)
    local = lax.rem(ids, per_owner)
    dx = lax.rem(lax.div(owner, NC * NZ) - my_x + NX, NX)
    dz = lax.rem(lax.rem(lax.div(owner, NC), NZ) - my_z + NZ, NZ)
    dc = lax.rem(lax.rem(owner, NC) - my_c + NC, NC)
    place = jnp.where(dz == 0, 0, jnp.where(dz <= NZ // 2, 2 * dz - 1, 2 * (NZ - dz)))
    offset = place * group + dx * NC + dc
    offset_f = jnp.broadcast_to(offset.astype(F32), (rows, rows))
    same = offset_f == offset_f.T
    earlier = lax.broadcasted_iota(jnp.int32, (rows, rows), 0) < lax.broadcasted_iota(jnp.int32, (rows, rows), 1)
    rank = jnp.sum(jnp.where(same & earlier, 1.0, 0.0), axis=0, keepdims=True).astype(jnp.int32)
    target = offset * (2 * CAP) + rank
    targets = jnp.concatenate([target, target + CAP], axis=1)

    at_offset = lax.broadcasted_iota(jnp.int32, (owners, rows), 0) == offset
    at_rank = lax.broadcasted_iota(jnp.int32, (128, rows), 0) == rank
    id_table = lax.dot_general(
        jnp.where(at_offset, 1.0, 0.0).astype(BF16),
        jnp.where(at_rank, (local + 1).astype(F32), 0.0).astype(BF16),
        (((1,), (1,)), ((), ())),
        preferred_element_type=F32,
    ) - 1.0
    for k in range(owners):
        id_send[k] = id_table[k : k + 1, :]
    id_recv[0] = id_table[0:1, :]

    pl.semaphore_wait(barrier, owners - 1 + NY - 1)

    slab = group * 2 * CAP

    for m in range(NZ):
        hit = lax.broadcasted_iota(jnp.int32, (slab, 2 * rows), 0) + m * slab == targets
        part = jnp.dot(jnp.where(hit, 1.0, 0.0).astype(BF16), halves[...], preferred_element_type=F32)
        send[m * group : (m + 1) * group] = part.astype(BF16).reshape(group, 2 * CAP, half)
        if m == 0:
            keys[0, 0] = send[0]

        @pl.loop(max(m * group, 1), (m + 1) * group)
        def _(k):
            pltpu.make_async_remote_copy(
                src_ref=send.at[k], dst_ref=keys.at[0, k],
                send_sem=row_send_sem, recv_sem=row_recv_sem.at[m],
                device_id=(ahead(k), my_y), device_id_type=MESH,
            ).start()

    @pl.loop(1, owners)
    def _(k):
        pltpu.make_async_remote_copy(
            src_ref=id_send.at[k], dst_ref=id_recv.at[k],
            send_sem=id_send_sem, recv_sem=id_recv_sem,
            device_id=(ahead(k), my_y), device_id_type=MESH,
        ).start()

    strip = min(128, owners * 2 * CAP)
    targets_f = jnp.broadcast_to(targets.astype(F32), (strip, 2 * rows)).T
    lanes = lax.broadcasted_iota(jnp.int32, (2 * rows, strip), 1).astype(F32)
    for j in range(owners * 2 * CAP // strip):
        turned[:, j * strip : (j + 1) * strip] = jnp.where(lanes + j * strip == targets_f, 1.0, 0.0).astype(BF16)

    def unpack(column, m):
        part = keys[column, m * group : (m + 1) * group].astype(F32)
        first = column * slots + m * chunk_rows
        table[first : first + chunk_rows, :half] = part[:, :CAP, :].reshape(chunk_rows, half).astype(BF16)
        table[first : first + chunk_rows, half:] = part[:, CAP:, :].reshape(chunk_rows, half).astype(BF16)

    def chunk(column, m):
        return keys.at[column, pl.ds(m * group, group)]

    def relay(m):
        wait_bytes(chunk(1, m), y_recv_sem.at[0, m])
        wait_bytes(chunk(3, m), y_recv_sem.at[1, m])
        source, to = (1, y_right) if m % 2 == 0 else (3, y_left)
        pltpu.make_async_remote_copy(
            src_ref=chunk(source, m), dst_ref=chunk(2, m),
            send_sem=relay_send_sem, recv_sem=far_recv_sem.at[m],
            device_id=(me, to), device_id_type=MESH,
        ).start()
        unpack(1, m)
        unpack(3, m)

    for m in range(NZ):
        arriving = keys.at[0, pl.ds(1, group - 1)] if m == 0 else chunk(0, m)
        wait_bytes(arriving, row_recv_sem.at[m])
        for way, to, column, sem in ((0, y_right, 1, right_send_sem), (1, y_left, 3, left_send_sem)):
            pltpu.make_async_remote_copy(
                src_ref=chunk(0, m), dst_ref=chunk(column, m),
                send_sem=sem, recv_sem=y_recv_sem.at[way, m],
                device_id=(me, to), device_id_type=MESH,
            ).start()
        unpack(0, m)
        if m == 1:
            wait_bytes(id_recv.at[pl.ds(1, owners - 1)], id_recv_sem)
            got = jnp.concatenate([id_recv[k] for k in range(owners)], axis=0)
            spread = (
                lax.broadcasted_iota(jnp.int32, (128, slots), 0)
                == lax.rem(lax.broadcasted_iota(jnp.int32, (128, slots), 1), CAP)
            )
            wide = jnp.dot(got.astype(BF16), jnp.where(spread, 1.0, 0.0).astype(BF16), preferred_element_type=F32)
            own = (
                lax.broadcasted_iota(jnp.int32, (owners, slots), 0)
                == lax.div(lax.broadcasted_iota(jnp.int32, (owners, slots), 1), CAP)
            )
            key_ids[0] = jnp.sum(jnp.where(own, wide, 0.0), axis=0, keepdims=True)
            for n, (to, column) in enumerate(((y_right, 1), (y_left, 3), (y_far, 2))):
                pltpu.make_async_remote_copy(
                    src_ref=key_ids.at[0], dst_ref=key_ids.at[column],
                    send_sem=kid_send_sem.at[n], recv_sem=kid_recv_sem.at[n],
                    device_id=(me, to), device_id_type=MESH,
                ).start()
        if m >= 1:
            relay(m - 1)
    relay(NZ - 1)

    for n, column in enumerate((1, 3, 2)):
        wait_bytes(key_ids.at[column], kid_recv_sem.at[n])

    query_id = jnp.broadcast_to(key_ids[0], (128, slots)).T[:, 0:1]
    query_temp = jnp.ones_like(query_id)
    for c in range(per_owner):
        query_temp = jnp.where(query_id == float(c), temp_ref[c], query_temp)
    query_id = jnp.where(query_id < 0.0, -2.0, query_id)

    block = min(256, slots)
    best = [jnp.full((block, 1), LOWEST, F32) for _ in range(slots // block)]
    for column in (0, 1, 3, 2):
        if column == 2:
            for m in range(NZ):
                wait_bytes(chunk(2, m), far_recv_sem.at[m])
                unpack(2, m)
        for b in range(slots // block):
            cosine = lax.dot_general(
                table[b * block : (b + 1) * block, :],
                table[column * slots : (column + 1) * slots, :],
                (((1,), (1,)), ((), ())),
                preferred_element_type=F32,
            )
            allowed = query_id[b * block : (b + 1) * block] == key_ids[column]
            if column == 0:
                allowed &= (
                    lax.broadcasted_iota(jnp.int32, (block, slots), 0) + b * block
                    != lax.broadcasted_iota(jnp.int32, (block, slots), 1)
                )
            score = jnp.where(allowed, cosine * query_temp[b * block : (b + 1) * block], LOWEST)
            scores[b * block : (b + 1) * block, column * slots : (column + 1) * slots] = score
            best[b] = jnp.maximum(best[b], jnp.max(score, axis=1, keepdims=True))

    per_block = block // CAP
    for b in range(slots // block - 1, -1, -1):
        here = pl.ds(b * block, block)
        close = best[b] / query_temp[b * block : (b + 1) * block]
        lane = lax.broadcasted_iota(jnp.int32, (block, 128), 1)
        rank_of = lax.rem(lax.broadcasted_iota(jnp.int32, (block, 128), 0), CAP)
        spread_close = jnp.sum(jnp.where(lane == rank_of, close, 0.0).reshape(per_block, CAP, 128), axis=1)
        for k in range(per_block):
            sim_send[b * per_block + k] = spread_close[k : k + 1, :]
        total = jnp.zeros((block, 1), F32)
        for column in range(NY):
            weight = jnp.exp(scores[here, column * slots : (column + 1) * slots] - best[b])
            total += jnp.sum(weight, axis=1, keepdims=True)
            weights[:, column * slots : (column + 1) * slots] = weight.astype(BF16)
        for h in range(2):
            summed = jnp.dot(weights[...], table[:, h * half : (h + 1) * half], preferred_element_type=F32)
            near = (summed / total).reshape(per_block, CAP, half)
            if h == 0:
                left = near
        outs[pl.ds(b * per_block, per_block)] = jnp.concatenate([left, near], axis=1).astype(BF16)
        if b == 0:
            back[0] = outs[0]
            sim_recv[0] = sim_send[0]

        @pl.loop(max(b * per_block, 1), (b + 1) * per_block)
        def _(k):
            to = behind(k)
            pltpu.make_async_remote_copy(
                src_ref=outs.at[k], dst_ref=back.at[k],
                send_sem=back_send_sem, recv_sem=back_recv_sem,
                device_id=(to, my_y), device_id_type=MESH,
            ).start()
            pltpu.make_async_remote_copy(
                src_ref=sim_send.at[k], dst_ref=sim_recv.at[k],
                send_sem=sim_send_sem, recv_sem=sim_recv_sem,
                device_id=(to, my_y), device_id_type=MESH,
            ).start()

    others = pl.ds(1, owners - 1)
    wait_bytes(sim_recv.at[others], sim_recv_sem)
    got = jnp.concatenate([sim_recv[k] for k in range(owners)], axis=0)
    picked = lax.dot_general(
        got, jnp.where(at_offset, 1.0, 0.0), (((0,), (0,)), ((), ())),
        preferred_element_type=F32, precision=lax.Precision.HIGHEST,
    )
    sim_ref[...] = jnp.sum(jnp.where(at_rank, picked, 0.0), axis=0, keepdims=True)

    wait_bytes(back.at[others], back_recv_sem)
    returned = jnp.dot(
        turned[...], back[...].reshape(owners * 2 * CAP, half), preferred_element_type=F32
    )
    out_ref[:, :half] = unit[:, :half] - returned[:rows]
    out_ref[:, half:] = unit[:, half:] - returned[rows:]

    wait_bytes(send.at[others], row_send_sem)
    wait_bytes(id_send.at[others], id_send_sem)
    wait_bytes(outs.at[others], back_send_sem)
    wait_bytes(sim_send.at[others], sim_send_sem)
    wait_bytes(keys.at[0], right_send_sem)
    wait_bytes(keys.at[0], left_send_sem)
    wait_bytes(keys.at[2], relay_send_sem)
    for n in range(3):
        wait_bytes(key_ids.at[0], kid_send_sem.at[n])


def per_device(embeds, cluster_ids, inv_temp):
    rows, width = embeds.shape
    group = NX * NC
    owners = group * NZ
    slots = owners * CAP
    half = width // 2
    block = min(256, slots)
    DMA = pltpu.SemaphoreType.DMA
    vmem = pl.BlockSpec(memory_space=pltpu.VMEM)
    residual, similarity = pl.pallas_call(
        kernel,
        out_shape=(jax.ShapeDtypeStruct((rows, width), F32), jax.ShapeDtypeStruct((1, rows), F32)),
        in_specs=[vmem, vmem, pl.BlockSpec(memory_space=pltpu.SMEM)],
        out_specs=(vmem, vmem),
        scratch_shapes=[
            pltpu.VMEM((rows, width), F32),
            pltpu.VMEM((2 * rows, half), BF16),
            pltpu.VMEM((owners, 2 * CAP, half), BF16),
            pltpu.VMEM((NY, owners, 2 * CAP, half), BF16),
            pltpu.VMEM((NY * slots, width), BF16),
            pltpu.VMEM((slots, NY * slots), F32),
            pltpu.VMEM((block, NY * slots), BF16),
            pltpu.VMEM((owners, 2 * CAP, half), BF16),
            pltpu.VMEM((owners, 2 * CAP, half), BF16),
            pltpu.VMEM((2 * rows, owners * 2 * CAP), BF16),
            pltpu.VMEM((owners, 1, 128), F32),
            pltpu.VMEM((owners, 1, 128), F32),
            pltpu.VMEM((NY, 1, slots), F32),
            pltpu.VMEM((owners, 1, 128), F32),
            pltpu.VMEM((owners, 1, 128), F32),
            DMA, DMA((NZ,)), DMA, DMA, DMA,
            DMA((2, NZ)), DMA((NZ,)), DMA, DMA, DMA((3,)), DMA((3,)),
            DMA, DMA, DMA, DMA,
        ],
        compiler_params=pltpu.CompilerParams(
            collective_id=0, has_side_effects=True, vmem_limit_bytes=48 * 1024 * 1024
        ),
    )(cluster_ids.reshape(1, rows), embeds, inv_temp)
    return residual, similarity.reshape(rows)


def solution(mesh):
    in_specs = (P(("dp", "clus"), None), P(("dp", "clus")), P("dp"))
    out_specs = (P(("dp", "clus"), None), P(("dp", "clus")))
    return jax.shard_map(
        per_device, mesh=mesh, in_specs=in_specs, out_specs=out_specs, check_vma=False
    )
```

```python
import functools

import jax
import jax.numpy as jnp
from jax import lax
from jax.experimental import pallas as pl
from jax.experimental.pallas import tpu as pltpu
from jax.sharding import PartitionSpec as P

NX, NZ, NC, NY = 4, 8, 2, 4
CAP = 8
LOWEST = -1e30
AHEAD = 4
MESH = pl.DeviceIdType.MESH
F32 = jnp.float32
BF16 = jnp.bfloat16


def wait_bytes(ref, sem):
    pltpu.make_async_copy(ref, ref, sem).wait()


def kernel(
    ids_hbm, x_hbm, temp_ref, out_ref, sim_ref,
    ids_ref, x_ref, unit, halves, send, keys, table, scores, weights, outs, back, turned,
    raw, key_ids, sim_send, sim_mid, sim_recv,
    load_sem, ready_sem, row_send_sem, row_recv_sem, y_send_sem, relay_send_sem,
    y_recv_sem, far_recv_sem, raw_send_sem, raw_z_sem, raw_plane_sem, raw_y_sem,
    back_send_sem, back_recv_sem, sim_send_sem, sim_z_sem, sim_plane_sem,
):
    group = NX * NC
    owners = group * NZ
    rows, width = x_ref.shape
    half = width // 2
    slots = owners * CAP
    per_owner = temp_ref.shape[0]
    chunk_rows = group * CAP
    near_group = group // 2

    me = lax.axis_index("dp")
    my_y = lax.axis_index("clus")
    my_c = lax.rem(me, NC)
    my_z = lax.rem(lax.div(me, NC), NZ)
    my_x = lax.div(me, NC * NZ)
    y_right = lax.rem(my_y + 1, NY)
    y_left = lax.rem(my_y + NY - 1, NY)
    y_far = lax.rem(my_y + 2, NY)

    def swap(m):
        return m if m == 0 or m == NZ - 1 else (m + 1 if m % 2 else m - 1)

    def shift_of(m, g):
        far = lax.div(m + 1, 2)
        odd = lax.rem(m + lax.div(g, near_group), 2)
        dz = odd * far + (1 - odd) * lax.rem(NZ - far, NZ)
        return lax.div(g, NC), dz, lax.rem(g, NC)

    def ahead(m, g):
        dx, dz, dc = shift_of(m, g)
        x, z, c = lax.rem(my_x + dx, NX), lax.rem(my_z + dz, NZ), lax.rem(my_c + dc, NC)
        return ((x * NZ + z) * NC + c, my_y)

    def behind(m, g):
        dx, dz, dc = shift_of(m, g)
        x, z, c = lax.rem(my_x + NX - dx, NX), lax.rem(my_z + NZ - dz, NZ), lax.rem(my_c + NC - dc, NC)
        return ((x * NZ + z) * NC + c, my_y)

    def plane(g):
        x, c = lax.rem(my_x + lax.div(g, NC), NX), lax.rem(my_c + lax.rem(g, NC), NC)
        return ((x * NZ + my_z) * NC + c, my_y)

    def plane_back(g):
        x, c = lax.rem(my_x + NX - lax.div(g, NC), NX), lax.rem(my_c + NC - lax.rem(g, NC), NC)
        return ((x * NZ + my_z) * NC + c, my_y)

    def push(src, dst, send_sem, recv_sem, to):
        pltpu.make_async_remote_copy(
            src_ref=src, dst_ref=dst, send_sem=send_sem, recv_sem=recv_sem,
            device_id=to, device_id_type=MESH,
        ).start()

    loads = [
        pltpu.make_async_copy(x_hbm, x_ref, load_sem.at[0]),
        pltpu.make_async_copy(ids_hbm, ids_ref, load_sem.at[1]),
    ]
    for load in loads:
        load.start()

    barrier = pltpu.get_barrier_semaphore()

    @pl.loop(1, group)
    def _(g):
        pl.semaphore_signal(barrier, inc=1, device_id=plane(g), device_id_type=MESH)

    @pl.loop(1, NZ)
    def _(m):
        pl.semaphore_signal(barrier, inc=1, device_id=ahead(m, 0), device_id_type=MESH)

    for y in (y_right, y_left, y_far):
        pl.semaphore_signal(barrier, inc=1, device_id=(me, y), device_id_type=MESH)

    loads[1].wait()
    loads[0].wait()
    x = x_ref[...]
    unit_rows = x * lax.rsqrt(jnp.sum(x * x, axis=1, keepdims=True) + 1e-06)
    unit[...] = unit_rows
    packed = unit_rows.astype(BF16)
    halves[:rows, :] = packed[:, :half]
    halves[rows:, :] = packed[:, half:]

    ids = ids_ref[...]
    owner = lax.div(ids, per_owner)
    dx = lax.rem(lax.div(owner, NC * NZ) - my_x + NX, NX)
    dz = lax.rem(lax.rem(lax.div(owner, NC), NZ) - my_z + NZ, NZ)
    dc = lax.rem(lax.rem(owner, NC) - my_c + NC, NC)
    g_of = dx * NC + dc
    up = jnp.where(g_of < near_group, 2 * dz - 1, 2 * dz)
    down = jnp.where(g_of < near_group, 2 * (NZ - dz), 2 * (NZ - dz) - 1)
    place = jnp.where(dz == 0, 0, jnp.where(dz == NZ // 2, NZ - 1, jnp.where(dz < NZ // 2, up, down)))
    offset = place * group + g_of
    offset_f = jnp.broadcast_to(offset.astype(F32), (rows, rows))
    same = offset_f == offset_f.T
    earlier = lax.broadcasted_iota(jnp.int32, (rows, rows), 0) < lax.broadcasted_iota(jnp.int32, (rows, rows), 1)
    rank = jnp.sum(jnp.where(same & earlier, 1.0, 0.0), axis=0, keepdims=True).astype(jnp.int32)
    target = offset * (2 * CAP) + rank
    targets = jnp.concatenate([target, target + CAP], axis=1)
    raw[0, 0, 0] = ids

    slab = group * 2 * CAP

    def pack(m):
        hit = lax.broadcasted_iota(jnp.int32, (slab, 2 * rows), 0) + m * slab == targets
        part = jnp.dot(jnp.where(hit, 1.0, 0.0).astype(BF16), halves[...], preferred_element_type=F32)
        send[m * group : (m + 1) * group] = part.astype(BF16).reshape(group, 2 * CAP, half)
        if m == 0:
            keys[0, 0] = send[0]

    def ship(m):
        @pl.loop(1 if m == 0 else 0, group)
        def _(g):
            k = m * group + g
            push(send.at[k], keys.at[0, k], row_send_sem, row_recv_sem.at[m], ahead(m, g))

    pack(0)
    pl.semaphore_wait(barrier, group - 1 + NZ - 1 + NY - 1)

    @pl.loop(1, group)
    def _(g):
        pl.semaphore_signal(ready_sem, inc=1, device_id=plane(g), device_id_type=MESH)

    ship(0)
    for m in range(1, min(AHEAD, NZ)):
        pack(m)
    pl.semaphore_wait(ready_sem, group - 1)
    for m in range(1, min(AHEAD, NZ)):
        ship(m)

    @pl.loop(1, NZ)
    def _(m):
        push(raw.at[0, 0, 0], raw.at[0, m, 0], raw_send_sem.at[0], raw_z_sem, ahead(m, 0))

    def raw_plane():
        wait_bytes(raw.at[0, pl.ds(1, NZ - 1), 0], raw_z_sem)

        @pl.loop(1, group)
        def _(g):
            push(raw.at[0, :, 0], raw.at[0, :, g], raw_send_sem.at[1], raw_plane_sem, plane(g))

    def raw_y():
        wait_bytes(raw.at[0, :, pl.ds(1, group - 1)], raw_plane_sem)
        for n, (to, column) in enumerate(((y_right, 1), (y_left, 3), (y_far, 2))):
            push(raw.at[0], raw.at[column], raw_send_sem.at[2 + n], raw_y_sem.at[n], (me, to))

    def read_ids(column):
        parts = []
        for m in range(NZ):
            parts += [raw[column, m, :near_group], raw[column, swap(m), near_group:]]
        ids_of = jnp.broadcast_to(jnp.concatenate(parts, axis=0), (owners, CAP, rows)).reshape(slots, rows)
        mine = lax.div(ids_of, per_owner) == me
        below = (
            lax.broadcasted_iota(jnp.int32, (rows, rows), 0) < lax.broadcasted_iota(jnp.int32, (rows, rows), 1)
        )
        ranks = jnp.dot(
            jnp.where(mine, 1.0, 0.0).astype(BF16), jnp.where(below, 1.0, 0.0).astype(BF16),
            preferred_element_type=F32,
        )
        slot_rank = lax.rem(lax.broadcasted_iota(jnp.int32, (slots, rows), 0), CAP).astype(F32)
        value = (lax.rem(ids_of, per_owner) + 1).astype(F32)
        chosen = jnp.where(mine & (ranks == slot_rank), value, 0.0).astype(BF16)
        key_ids[column] = lax.dot_general(
            jnp.ones((8, rows), BF16), chosen, (((1,), (1,)), ((), ())), preferred_element_type=F32
        ) - 1.0
        return chosen

    strip = min(128, owners * 2 * CAP)
    targets_f = jnp.broadcast_to(targets.astype(F32), (strip, 2 * rows)).T
    lanes = lax.broadcasted_iota(jnp.int32, (2 * rows, strip), 1).astype(F32)
    for j in range(owners * 2 * CAP // strip):
        turned[:, j * strip : (j + 1) * strip] = jnp.where(lanes + j * strip == targets_f, 1.0, 0.0).astype(BF16)

    def unpack(column, m):
        part = keys[column, m * group : (m + 1) * group].astype(F32)
        first = column * slots + m * chunk_rows
        table[first : first + chunk_rows, :half] = part[:, :CAP, :].reshape(chunk_rows, half).astype(BF16)
        table[first : first + chunk_rows, half:] = part[:, CAP:, :].reshape(chunk_rows, half).astype(BF16)

    def chunk(column, m):
        return keys.at[column, pl.ds(m * group, group)]

    def part_of(column, m, part):
        return keys.at[column, pl.ds(m * group + part * near_group, near_group)]

    def relay(m):
        for way, to, column in ((0, y_right, 1), (1, y_left, 3)):
            wait_bytes(chunk(column, m), y_recv_sem.at[way, m])
            push(part_of(column, m, way), part_of(2, m, way), relay_send_sem.at[way], far_recv_sem.at[way, m], (me, to))
        unpack(1, m)
        unpack(3, m)

    for m in range(NZ):
        if m + AHEAD < NZ:
            pack(m + AHEAD)
            ship(m + AHEAD)
        arriving = keys.at[0, pl.ds(1, group - 1)] if m == 0 else chunk(0, m)
        wait_bytes(arriving, row_recv_sem.at[m])
        push(chunk(0, m), chunk(1, m), y_send_sem.at[0], y_recv_sem.at[0, m], (me, y_right))
        push(chunk(0, m), chunk(3, m), y_send_sem.at[1], y_recv_sem.at[1, m], (me, y_left))
        unpack(0, m)
        if m == min(1, NZ - 1):
            raw_plane()
        if m >= 1:
            relay(m - 1)
        if m == min(3, NZ - 1):
            raw_y()
        if m >= 2:
            for way in range(2):
                wait_bytes(part_of(2, m - 2, way), far_recv_sem.at[way, m - 2])
            unpack(2, m - 2)
    relay(NZ - 1)

    chosen = read_ids(0)
    query_id = jnp.dot(chosen, jnp.ones((rows, 128), BF16), preferred_element_type=F32)[:, 0:1] - 1.0
    query_temp = jnp.ones_like(query_id)
    for c in range(per_owner):
        query_temp = jnp.where(query_id == float(c), temp_ref[c], query_temp)
    query_id = jnp.where(query_id < 0.0, -2.0, query_id)
    for n, column in enumerate((1, 3, 2)):
        wait_bytes(raw.at[column], raw_y_sem.at[n])
        read_ids(column)

    block = min(256, slots)
    best = [jnp.full((block, 1), LOWEST, F32) for _ in range(slots // block)]
    for column in (0, 1, 3, 2):
        if column == 2:
            for m in range(max(NZ - 2, 0), NZ):
                for way in range(2):
                    wait_bytes(part_of(2, m, way), far_recv_sem.at[way, m])
                unpack(2, m)
        for b in range(slots // block - 1, -1, -1):
            cosine = lax.dot_general(
                table[b * block : (b + 1) * block, :],
                table[column * slots : (column + 1) * slots, :],
                (((1,), (1,)), ((), ())),
                preferred_element_type=F32,
            )
            allowed = query_id[b * block : (b + 1) * block] == key_ids[column, 0:1, :]
            if column == 0:
                allowed &= (
                    lax.broadcasted_iota(jnp.int32, (block, slots), 0) + b * block
                    != lax.broadcasted_iota(jnp.int32, (block, slots), 1)
                )
            score = jnp.where(allowed, cosine * query_temp[b * block : (b + 1) * block], LOWEST)
            scores[b * block : (b + 1) * block, column * slots : (column + 1) * slots] = score
            best[b] = jnp.maximum(best[b], jnp.max(score, axis=1, keepdims=True))

    per_block = block // CAP
    for b in range(slots // block):
        close = best[b] / query_temp[b * block : (b + 1) * block]
        lane = lax.broadcasted_iota(jnp.int32, (block, 128), 1)
        rank_of = lax.rem(lax.broadcasted_iota(jnp.int32, (block, 128), 0), CAP)
        spread_close = jnp.sum(jnp.where(lane == rank_of, close, 0.0).reshape(per_block, CAP, 128), axis=1)
        for j in range(per_block):
            m, g = divmod(b * per_block + j, group)
            sim_send[m if g < near_group else swap(m), g] = spread_close[j : j + 1, :]
    sim_mid[0] = sim_send[0]

    @pl.loop(1, NZ)
    def _(m):
        push(sim_send.at[m], sim_mid.at[m], sim_send_sem.at[0], sim_z_sem, behind(m, 0))

    for b in range(slots // block - 1, -1, -1):
        here = pl.ds(b * block, block)
        total = jnp.zeros((block, 1), F32)
        for column in range(NY):
            weight = jnp.exp(scores[here, column * slots : (column + 1) * slots] - best[b])
            total += jnp.sum(weight, axis=1, keepdims=True)
            weights[:, column * slots : (column + 1) * slots] = weight.astype(BF16)
        near = []
        for h in range(2):
            summed = jnp.dot(weights[...], table[:, h * half : (h + 1) * half], preferred_element_type=F32)
            near.append((summed / total).reshape(per_block, CAP, half))
        outs[pl.ds(b * per_block, per_block)] = jnp.concatenate(near, axis=1).astype(BF16)
        if b == 0:
            back[0] = outs[0]

        for m in range((b + 1) * per_block // group - 1, b * per_block // group - 1, -1):
            @pl.loop(1 if m == 0 else 0, group)
            def _(g):
                k = m * group + g
                push(outs.at[k], back.at[k], back_send_sem, back_recv_sem, behind(m, g))

        if b == slots // block - 1:
            wait_bytes(sim_mid.at[pl.ds(1, NZ - 1)], sim_z_sem)
            sim_recv[:, 0] = sim_mid[:, 0]

            @pl.loop(1, group)
            def _(g):
                push(sim_mid.at[:, g], sim_recv.at[:, g], sim_send_sem.at[1], sim_plane_sem, plane_back(g))

    others = pl.ds(1, owners - 1)
    wait_bytes(sim_recv.at[:, pl.ds(1, group - 1)], sim_plane_sem)
    got = []
    for k in range(owners):
        m, g = divmod(k, group)
        got.append(sim_recv[m if g < near_group else swap(m), g])
    at_offset = lax.broadcasted_iota(jnp.int32, (owners, rows), 0) == offset
    at_rank = lax.broadcasted_iota(jnp.int32, (128, rows), 0) == rank
    picked = lax.dot_general(
        jnp.concatenate(got, axis=0), jnp.where(at_offset, 1.0, 0.0), (((0,), (0,)), ((), ())),
        preferred_element_type=F32, precision=lax.Precision.HIGHEST,
    )
    sim_ref[...] = jnp.sum(jnp.where(at_rank, picked, 0.0), axis=0, keepdims=True)

    wait_bytes(send.at[others], row_send_sem)
    wait_bytes(sim_send.at[pl.ds(1, NZ - 1)], sim_send_sem.at[0])
    wait_bytes(sim_mid.at[:, pl.ds(1, group - 1)], sim_send_sem.at[1])
    wait_bytes(raw.at[0, pl.ds(1, NZ - 1), 0], raw_send_sem.at[0])
    wait_bytes(raw.at[0, :, pl.ds(1, group - 1)], raw_send_sem.at[1])
    for n in range(3):
        wait_bytes(raw.at[0], raw_send_sem.at[2 + n])
    for way in range(2):
        wait_bytes(keys.at[0], y_send_sem.at[way])
        wait_bytes(keys.at[0, pl.ds(0, owners // 2)], relay_send_sem.at[way])

    wait_bytes(back.at[others], back_recv_sem)
    returned = jnp.dot(
        turned[...], back[...].reshape(owners * 2 * CAP, half), preferred_element_type=F32
    )
    out_ref[:, :half] = unit[:, :half] - returned[:rows]
    out_ref[:, half:] = unit[:, half:] - returned[rows:]
    wait_bytes(outs.at[others], back_send_sem)


def per_device(embeds, cluster_ids, inv_temp):
    rows, width = embeds.shape
    group = NX * NC
    owners = group * NZ
    slots = owners * CAP
    half = width // 2
    block = min(256, slots)
    DMA = pltpu.SemaphoreType.DMA
    vmem = pl.BlockSpec(memory_space=pltpu.VMEM)
    hbm = pl.BlockSpec(memory_space=pltpu.HBM)
    residual, similarity = pl.pallas_call(
        kernel,
        out_shape=(jax.ShapeDtypeStruct((rows, width), F32), jax.ShapeDtypeStruct((1, rows), F32)),
        in_specs=[hbm, hbm, pl.BlockSpec(memory_space=pltpu.SMEM)],
        out_specs=(vmem, vmem),
        scratch_shapes=[
            pltpu.VMEM((1, rows), jnp.int32),
            pltpu.VMEM((rows, width), F32),
            pltpu.VMEM((rows, width), F32),
            pltpu.VMEM((2 * rows, half), BF16),
            pltpu.VMEM((owners, 2 * CAP, half), BF16),
            pltpu.VMEM((NY, owners, 2 * CAP, half), BF16),
            pltpu.VMEM((NY * slots, width), BF16),
            pltpu.VMEM((slots, NY * slots), F32),
            pltpu.VMEM((block, NY * slots), BF16),
            pltpu.VMEM((owners, 2 * CAP, half), BF16),
            pltpu.VMEM((owners, 2 * CAP, half), BF16),
            pltpu.VMEM((2 * rows, owners * 2 * CAP), BF16),
            pltpu.VMEM((NY, NZ, group, 1, rows), jnp.int32),
            pltpu.VMEM((NY, 8, slots), F32),
            pltpu.VMEM((NZ, group, 1, 128), F32),
            pltpu.VMEM((NZ, group, 1, 128), F32),
            pltpu.VMEM((NZ, group, 1, 128), F32),
            DMA((2,)), pltpu.SemaphoreType.REGULAR, DMA, DMA((NZ,)), DMA((2,)), DMA((2,)),
            DMA((2, NZ)), DMA((2, NZ)), DMA((5,)), DMA, DMA, DMA((3,)),
            DMA, DMA, DMA((2,)), DMA, DMA,
        ],
        compiler_params=pltpu.CompilerParams(
            collective_id=0, has_side_effects=True, vmem_limit_bytes=48 * 1024 * 1024
        ),
    )(cluster_ids.reshape(1, rows), embeds, inv_temp)
    return residual, similarity.reshape(rows)


def solution(mesh):
    in_specs = (P(("dp", "clus"), None), P(("dp", "clus")), P("dp"))
    out_specs = (P(("dp", "clus"), None), P(("dp", "clus")))
    return jax.shard_map(
        per_device, mesh=mesh, in_specs=in_specs, out_specs=out_specs, check_vma=False
    )
```

```python
import functools

import jax
import jax.numpy as jnp
from jax import lax
from jax.experimental import pallas as pl
from jax.experimental.pallas import tpu as pltpu
from jax.sharding import PartitionSpec as P

NX, NZ, NC, NY = 4, 8, 2, 4
CAP = 8
LOWEST = -1e30
AHEAD = 2
MESH = pl.DeviceIdType.MESH
F32 = jnp.float32
BF16 = jnp.bfloat16


def wait_bytes(ref, sem):
    pltpu.make_async_copy(ref, ref, sem).wait()


def kernel(
    ids_hbm, x_hbm, temp_hbm, out_ref, sim_ref,
    ids_ref, x_ref, temp_ref, unit, halves, send, keys, table, scores, weights, outs, back, turned,
    raw, key_ids, sim_send, sim_mid, sim_recv,
    load_sem, ready_sem, row_send_sem, row_recv_sem, y_send_sem, relay_send_sem,
    y_recv_sem, far_recv_sem, raw_send_sem, raw_z_sem, raw_plane_sem, raw_y_sem,
    back_send_sem, back_recv_sem, sim_send_sem, sim_z_sem, sim_plane_sem,
):
    group = NX * NC
    owners = group * NZ
    rows, width = x_ref.shape
    half = width // 2
    slots = owners * CAP
    per_owner = temp_ref.shape[0]
    chunk_rows = group * CAP
    near_group = group // 2

    me = lax.axis_index("dp")
    my_y = lax.axis_index("clus")
    my_c = lax.rem(me, NC)
    my_z = lax.rem(lax.div(me, NC), NZ)
    my_x = lax.div(me, NC * NZ)
    y_right = lax.rem(my_y + 1, NY)
    y_left = lax.rem(my_y + NY - 1, NY)
    y_far = lax.rem(my_y + 2, NY)

    def swap(m):
        return m if m == 0 or m == NZ - 1 else (m + 1 if m % 2 else m - 1)

    def shift_of(m, g):
        far = lax.div(m + 1, 2)
        odd = lax.rem(m + lax.div(g, near_group), 2)
        dz = odd * far + (1 - odd) * lax.rem(NZ - far, NZ)
        return lax.div(g, NC), dz, lax.rem(g, NC)

    def ahead(m, g):
        dx, dz, dc = shift_of(m, g)
        x, z, c = lax.rem(my_x + dx, NX), lax.rem(my_z + dz, NZ), lax.rem(my_c + dc, NC)
        return ((x * NZ + z) * NC + c, my_y)

    def behind(m, g):
        dx, dz, dc = shift_of(m, g)
        x, z, c = lax.rem(my_x + NX - dx, NX), lax.rem(my_z + NZ - dz, NZ), lax.rem(my_c + NC - dc, NC)
        return ((x * NZ + z) * NC + c, my_y)

    def plane(g):
        x, c = lax.rem(my_x + lax.div(g, NC), NX), lax.rem(my_c + lax.rem(g, NC), NC)
        return ((x * NZ + my_z) * NC + c, my_y)

    def plane_back(g):
        x, c = lax.rem(my_x + NX - lax.div(g, NC), NX), lax.rem(my_c + NC - lax.rem(g, NC), NC)
        return ((x * NZ + my_z) * NC + c, my_y)

    def push(src, dst, send_sem, recv_sem, to):
        pltpu.make_async_remote_copy(
            src_ref=src, dst_ref=dst, send_sem=send_sem, recv_sem=recv_sem,
            device_id=to, device_id_type=MESH,
        ).start()

    loads = [
        pltpu.make_async_copy(x_hbm, x_ref, load_sem.at[0]),
        pltpu.make_async_copy(ids_hbm, ids_ref, load_sem.at[1]),
        pltpu.make_async_copy(temp_hbm, temp_ref, load_sem.at[2]),
    ]
    for load in loads:
        load.start()

    barrier = pltpu.get_barrier_semaphore()

    @pl.loop(1, group)
    def _(g):
        pl.semaphore_signal(barrier, inc=1, device_id=plane(g), device_id_type=MESH)

    @pl.loop(1, NZ)
    def _(m):
        pl.semaphore_signal(barrier, inc=1, device_id=ahead(m, 0), device_id_type=MESH)

    for y in (y_right, y_left, y_far):
        pl.semaphore_signal(barrier, inc=1, device_id=(me, y), device_id_type=MESH)

    for load in loads:
        load.wait()
    x = x_ref[...]
    unit_rows = x * lax.rsqrt(jnp.sum(x * x, axis=1, keepdims=True) + 1e-06)
    unit[...] = unit_rows
    packed = unit_rows.astype(BF16)
    halves[:rows, :] = packed[:, :half]
    halves[rows:, :] = packed[:, half:]

    ids = ids_ref[...]
    owner = lax.div(ids, per_owner)
    dx = lax.rem(lax.div(owner, NC * NZ) - my_x + NX, NX)
    dz = lax.rem(lax.rem(lax.div(owner, NC), NZ) - my_z + NZ, NZ)
    dc = lax.rem(lax.rem(owner, NC) - my_c + NC, NC)
    g_of = dx * NC + dc
    up = jnp.where(g_of < near_group, 2 * dz - 1, 2 * dz)
    down = jnp.where(g_of < near_group, 2 * (NZ - dz), 2 * (NZ - dz) - 1)
    place = jnp.where(dz == 0, 0, jnp.where(dz == NZ // 2, NZ - 1, jnp.where(dz < NZ // 2, up, down)))
    offset = place * group + g_of
    offset_f = jnp.broadcast_to(offset.astype(F32), (rows, rows))
    same = offset_f == offset_f.T
    earlier = lax.broadcasted_iota(jnp.int32, (rows, rows), 0) < lax.broadcasted_iota(jnp.int32, (rows, rows), 1)
    rank = jnp.sum(jnp.where(same & earlier, 1.0, 0.0), axis=0, keepdims=True).astype(jnp.int32)
    target = offset * (2 * CAP) + rank
    targets = jnp.concatenate([target, target + CAP], axis=1)
    raw[0, 0, 0] = ids

    slab = group * 2 * CAP

    def pack(m):
        hit = lax.broadcasted_iota(jnp.int32, (slab, 2 * rows), 0) + m * slab == targets
        part = jnp.dot(jnp.where(hit, 1.0, 0.0).astype(BF16), halves[...], preferred_element_type=F32)
        send[m * group : (m + 1) * group] = part.astype(BF16).reshape(group, 2 * CAP, half)
        if m == 0:
            keys[0, 0] = send[0]

    def ship(m):
        @pl.loop(1 if m == 0 else 0, group)
        def _(g):
            k = m * group + g
            push(send.at[k], keys.at[0, k], row_send_sem, row_recv_sem.at[lax.div(g, near_group), m], ahead(m, g))

    pack(0)
    pl.semaphore_wait(barrier, group - 1 + NZ - 1 + NY - 1)

    @pl.loop(1, group)
    def _(g):
        pl.semaphore_signal(ready_sem, inc=1, device_id=plane(g), device_id_type=MESH)

    ship(0)
    for m in range(1, min(AHEAD, NZ)):
        pack(m)
    pl.semaphore_wait(ready_sem, group - 1)
    for m in range(1, min(AHEAD, NZ)):
        ship(m)

    @pl.loop(1, NZ)
    def _(m):
        push(raw.at[0, 0, 0], raw.at[0, m, 0], raw_send_sem.at[0], raw_z_sem, ahead(m, 0))

    def raw_plane():
        wait_bytes(raw.at[0, pl.ds(1, NZ - 1), 0], raw_z_sem)

        @pl.loop(1, group)
        def _(g):
            push(raw.at[0, :, 0], raw.at[0, :, g], raw_send_sem.at[1], raw_plane_sem, plane(g))

    def raw_y():
        wait_bytes(raw.at[0, :, pl.ds(1, group - 1)], raw_plane_sem)
        for n, (to, column) in enumerate(((y_right, 1), (y_left, 3), (y_far, 2))):
            push(raw.at[0], raw.at[column], raw_send_sem.at[2 + n], raw_y_sem.at[n], (me, to))

    def read_ids(column):
        parts = []
        for m in range(NZ):
            parts += [raw[column, m, :near_group], raw[column, swap(m), near_group:]]
        ids_of = jnp.broadcast_to(jnp.concatenate(parts, axis=0), (owners, CAP, rows)).reshape(slots, rows)
        mine = lax.div(ids_of, per_owner) == me
        below = (
            lax.broadcasted_iota(jnp.int32, (rows, rows), 0) < lax.broadcasted_iota(jnp.int32, (rows, rows), 1)
        )
        ranks = jnp.dot(
            jnp.where(mine, 1.0, 0.0).astype(BF16), jnp.where(below, 1.0, 0.0).astype(BF16),
            preferred_element_type=F32,
        )
        slot_rank = lax.rem(lax.broadcasted_iota(jnp.int32, (slots, rows), 0), CAP).astype(F32)
        value = (lax.rem(ids_of, per_owner) + 1).astype(F32)
        chosen = jnp.where(mine & (ranks == slot_rank), value, 0.0).astype(BF16)
        key_ids[column] = lax.dot_general(
            jnp.ones((8, rows), BF16), chosen, (((1,), (1,)), ((), ())), preferred_element_type=F32
        ) - 1.0
        return chosen

    strip = min(128, owners * 2 * CAP)
    targets_f = jnp.broadcast_to(targets.astype(F32), (strip, 2 * rows)).T
    lanes = lax.broadcasted_iota(jnp.int32, (2 * rows, strip), 1).astype(F32)
    for j in range(owners * 2 * CAP // strip):
        turned[:, j * strip : (j + 1) * strip] = jnp.where(lanes + j * strip == targets_f, 1.0, 0.0).astype(BF16)

    def unpack(column, m):
        part = keys[column, m * group : (m + 1) * group].astype(F32)
        first = column * slots + m * chunk_rows
        table[first : first + chunk_rows, :half] = part[:, :CAP, :].reshape(chunk_rows, half).astype(BF16)
        table[first : first + chunk_rows, half:] = part[:, CAP:, :].reshape(chunk_rows, half).astype(BF16)

    def chunk(column, m):
        return keys.at[column, pl.ds(m * group, group)]

    def part_of(column, m, part):
        return keys.at[column, pl.ds(m * group + part * near_group, near_group)]

    def relay(m):
        for way, to, column in ((0, y_right, 1), (1, y_left, 3)):
            wait_bytes(chunk(column, m), y_recv_sem.at[way, m])
            push(part_of(column, m, way), part_of(2, m, way), relay_send_sem.at[way], far_recv_sem.at[way, m], (me, to))
        unpack(1, m)
        unpack(3, m)

    block = min(256, slots)
    blocks = slots // block
    best = [jnp.full((block, 1), LOWEST, F32) for _ in range(blocks)]
    query = []

    def read_all_ids():
        chosen = read_ids(0)
        query_id = jnp.dot(chosen, jnp.ones((rows, 128), BF16), preferred_element_type=F32)[:, 0:1] - 1.0
        query_temp = jnp.ones_like(query_id)
        for c in range(per_owner):
            query_temp = jnp.where(query_id == float(c), temp_ref[c], query_temp)
        query.append(jnp.where(query_id < 0.0, -2.0, query_id))
        query.append(query_temp)
        for n, column in enumerate((1, 3, 2)):
            wait_bytes(raw.at[column], raw_y_sem.at[n])
            read_ids(column)

    def score(column, first, count):
        query_id, query_temp = query
        base = column * slots + first
        for b in range(blocks - 1, -1, -1):
            at = slice(b * block, (b + 1) * block)
            cosine = lax.dot_general(
                table[at, :], table[base : base + count, :], (((1,), (1,)), ((), ())),
                preferred_element_type=F32,
            )
            allowed = query_id[at] == key_ids[column, 0:1, first : first + count]
            if column == 0:
                allowed &= (
                    lax.broadcasted_iota(jnp.int32, (block, count), 0) + b * block
                    != lax.broadcasted_iota(jnp.int32, (block, count), 1) + first
                )
            scored = jnp.where(allowed, cosine * query_temp[at], LOWEST)
            scores[at, base : base + count] = scored
            best[b] = jnp.maximum(best[b], jnp.max(scored, axis=1, keepdims=True))

    def far(m):
        for way in range(2):
            wait_bytes(part_of(2, m, way), far_recv_sem.at[way, m])
        unpack(2, m)

    for m in range(NZ):
        if m + AHEAD < NZ:
            pack(m + AHEAD)
            ship(m + AHEAD)
        for part in range(2):
            first = m * group + part * near_group
            mine = 1 if first == 0 else 0
            if near_group > mine:
                wait_bytes(keys.at[0, pl.ds(first + mine, near_group - mine)], row_recv_sem.at[part, m])
            push(part_of(0, m, part), part_of(1, m, part), y_send_sem.at[0], y_recv_sem.at[0, m], (me, y_right))
            push(part_of(0, m, part), part_of(3, m, part), y_send_sem.at[1], y_recv_sem.at[1, m], (me, y_left))
        unpack(0, m)
        if m == min(1, NZ - 1):
            raw_plane()
        if m >= 1:
            relay(m - 1)
        if m == min(3, NZ - 1):
            raw_y()
        if m >= 2:
            far(m - 2)
        if m == min(5, NZ - 1):
            read_all_ids()
        if m == NZ - 1:
            score(0, 0, slots)
    relay(NZ - 1)
    score(1, 0, slots)
    score(3, 0, slots)
    half_slots = slots // 2
    late = range(max(NZ - 2, 0), NZ)
    for m in late:
        if m < NZ // 2:
            far(m)
    score(2, 0, half_slots)
    for m in late:
        if m >= NZ // 2:
            far(m)
    score(2, half_slots, half_slots)
    query_temp = query[1]

    per_block = block // CAP

    def similarities():
        for b in range(slots // block):
            close = best[b] / query_temp[b * block : (b + 1) * block]
            lane = lax.broadcasted_iota(jnp.int32, (block, 128), 1)
            rank_of = lax.rem(lax.broadcasted_iota(jnp.int32, (block, 128), 0), CAP)
            spread_close = jnp.sum(jnp.where(lane == rank_of, close, 0.0).reshape(per_block, CAP, 128), axis=1)
            for j in range(per_block):
                m, g = divmod(b * per_block + j, group)
                sim_send[m if g < near_group else swap(m), g] = spread_close[j : j + 1, :]
        sim_mid[0] = sim_send[0]

        @pl.loop(1, NZ)
        def _(m):
            push(sim_send.at[m], sim_mid.at[m], sim_send_sem.at[0], sim_z_sem, behind(m, 0))


    def way_back(m):
        @pl.loop(1 if m == 0 else 0, group)
        def _(g):
            k = m * group + g
            push(outs.at[k], back.at[k], back_send_sem, back_recv_sem.at[back_part(m)], behind(m, g))

    def back_part(m):
        return m * chunk_rows // block

    for b in range(blocks - 1, -1, -1):
        here = pl.ds(b * block, block)
        total = jnp.zeros((block, 1), F32)
        for column in range(NY):
            weight = jnp.exp(scores[here, column * slots : (column + 1) * slots] - best[b])
            total += jnp.sum(weight, axis=1, keepdims=True)
            weights[:, column * slots : (column + 1) * slots] = weight.astype(BF16)
        near = []
        for h in range(2):
            summed = jnp.dot(weights[...], table[:, h * half : (h + 1) * half], preferred_element_type=F32)
            near.append((summed / total).reshape(per_block, CAP, half))
        outs[pl.ds(b * per_block, per_block)] = jnp.concatenate(near, axis=1).astype(BF16)
        if b == 0:
            back[0] = outs[0]
        if b == blocks - 2 or blocks == 1:
            if blocks == 1:
                similarities()
            wait_bytes(sim_mid.at[pl.ds(1, NZ - 1)], sim_z_sem)
            sim_recv[:, 0] = sim_mid[:, 0]

            @pl.loop(1, group)
            def _(g):
                push(sim_mid.at[:, g], sim_recv.at[:, g], sim_send_sem.at[1], sim_plane_sem, plane_back(g))

        chunks = list(range((b + 1) * per_block // group - 1, b * per_block // group - 1, -1))
        for n, m in enumerate(chunks):
            way_back(m)
            if n == 1 and b == blocks - 1 and blocks > 1:
                similarities()

    others = pl.ds(1, owners - 1)
    wait_bytes(sim_recv.at[:, pl.ds(1, group - 1)], sim_plane_sem)
    got = []
    for k in range(owners):
        m, g = divmod(k, group)
        got.append(sim_recv[m if g < near_group else swap(m), g])
    at_offset = lax.broadcasted_iota(jnp.int32, (owners, rows), 0) == offset
    at_rank = lax.broadcasted_iota(jnp.int32, (128, rows), 0) == rank
    picked = lax.dot_general(
        jnp.concatenate(got, axis=0), jnp.where(at_offset, 1.0, 0.0), (((0,), (0,)), ((), ())),
        preferred_element_type=F32, precision=lax.Precision.HIGHEST,
    )
    sim_ref[...] = jnp.sum(jnp.where(at_rank, picked, 0.0), axis=0, keepdims=True)

    wait_bytes(send.at[others], row_send_sem)
    wait_bytes(sim_send.at[pl.ds(1, NZ - 1)], sim_send_sem.at[0])
    wait_bytes(sim_mid.at[:, pl.ds(1, group - 1)], sim_send_sem.at[1])
    wait_bytes(raw.at[0, pl.ds(1, NZ - 1), 0], raw_send_sem.at[0])
    wait_bytes(raw.at[0, :, pl.ds(1, group - 1)], raw_send_sem.at[1])
    for n in range(3):
        wait_bytes(raw.at[0], raw_send_sem.at[2 + n])
    for way in range(2):
        wait_bytes(keys.at[0], y_send_sem.at[way])
        wait_bytes(keys.at[0, pl.ds(0, owners // 2)], relay_send_sem.at[way])

    span = 2 * block
    for b in range(blocks - 1, -1, -1):
        first = max(b * per_block, 1)
        wait_bytes(back.at[pl.ds(first, (b + 1) * per_block - first)], back_recv_sem.at[b])
        returned = jnp.dot(
            turned[:, b * span : (b + 1) * span],
            back[b * per_block : (b + 1) * per_block].reshape(span, half),
            preferred_element_type=F32,
        )
        if b > 0:
            unit[:, :half] -= returned[:rows]
            unit[:, half:] -= returned[rows:]
        else:
            out_ref[:, :half] = unit[:, :half] - returned[:rows]
            out_ref[:, half:] = unit[:, half:] - returned[rows:]
    wait_bytes(outs.at[others], back_send_sem)


def per_device(embeds, cluster_ids, inv_temp):
    rows, width = embeds.shape
    group = NX * NC
    owners = group * NZ
    slots = owners * CAP
    half = width // 2
    block = min(256, slots)
    DMA = pltpu.SemaphoreType.DMA
    vmem = pl.BlockSpec(memory_space=pltpu.VMEM)
    hbm = pl.BlockSpec(memory_space=pltpu.HBM)
    residual, similarity = pl.pallas_call(
        kernel,
        out_shape=(jax.ShapeDtypeStruct((rows, width), F32), jax.ShapeDtypeStruct((1, rows), F32)),
        in_specs=[hbm, hbm, hbm],
        out_specs=(vmem, vmem),
        scratch_shapes=[
            pltpu.VMEM((1, rows), jnp.int32),
            pltpu.VMEM((rows, width), F32),
            pltpu.SMEM(inv_temp.shape, F32),
            pltpu.VMEM((rows, width), F32),
            pltpu.VMEM((2 * rows, half), BF16),
            pltpu.VMEM((owners, 2 * CAP, half), BF16),
            pltpu.VMEM((NY, owners, 2 * CAP, half), BF16),
            pltpu.VMEM((NY * slots, width), BF16),
            pltpu.VMEM((slots, NY * slots), F32),
            pltpu.VMEM((block, NY * slots), BF16),
            pltpu.VMEM((owners, 2 * CAP, half), BF16),
            pltpu.VMEM((owners, 2 * CAP, half), BF16),
            pltpu.VMEM((2 * rows, owners * 2 * CAP), BF16),
            pltpu.VMEM((NY, NZ, group, 1, rows), jnp.int32),
            pltpu.VMEM((NY, 8, slots), F32),
            pltpu.VMEM((NZ, group, 1, 128), F32),
            pltpu.VMEM((NZ, group, 1, 128), F32),
            pltpu.VMEM((NZ, group, 1, 128), F32),
            DMA((3,)), pltpu.SemaphoreType.REGULAR, DMA, DMA((2, NZ)), DMA((2,)), DMA((2,)),
            DMA((2, NZ)), DMA((2, NZ)), DMA((5,)), DMA, DMA, DMA((3,)),
            DMA, DMA((2,)), DMA((2,)), DMA, DMA,
        ],
        compiler_params=pltpu.CompilerParams(
            collective_id=0, has_side_effects=True, vmem_limit_bytes=48 * 1024 * 1024
        ),
    )(*(pltpu.with_memory_space_constraint(a, pltpu.HBM) for a in (cluster_ids.reshape(1, rows), embeds, inv_temp)))
    return residual, similarity.reshape(rows)


def solution(mesh):
    in_specs = (P(("dp", "clus"), None), P(("dp", "clus")), P("dp"))
    out_specs = (P(("dp", "clus"), None), P(("dp", "clus")))
    return jax.shard_map(
        per_device, mesh=mesh, in_specs=in_specs, out_specs=out_specs, check_vma=False
    )
```

```python
import functools

import jax
import jax.numpy as jnp
from jax import lax
from jax.experimental import pallas as pl
from jax.experimental.pallas import tpu as pltpu
from jax.sharding import PartitionSpec as P

NX, NZ, NC, NY = 4, 8, 2, 4
CAP = 8
LOWEST = -1e30
FINE = 128
AHEAD = 3
MESH = pl.DeviceIdType.MESH
F32 = jnp.float32
BF16 = jnp.bfloat16


def wait_bytes(ref, sem):
    pltpu.make_async_copy(ref, ref, sem).wait()


def kernel(
    ids_hbm, x_hbm, temp_hbm, out_ref, sim_ref,
    ids_ref, x_ref, temp_ref, unit, halves, send, keys, table, scores, weights, outs, back, turned,
    raw, key_ids, sim_send, sim_mid, sim_recv,
    load_sem, ready_sem, row_send_sem, row_recv_sem, y_send_sem, relay_send_sem,
    y_recv_sem, far_recv_sem, raw_send_sem, raw_z_sem, raw_plane_sem, raw_y_sem,
    back_send_sem, back_recv_sem, sim_send_sem, sim_z_sem, sim_plane_sem,
):
    group = NX * NC
    owners = group * NZ
    rows, width = x_ref.shape
    half = width // 2
    slots = owners * CAP
    per_owner = temp_ref.shape[0]
    chunk_rows = group * CAP
    near_group = group // 2

    me = lax.axis_index("dp")
    my_y = lax.axis_index("clus")
    my_c = lax.rem(me, NC)
    my_z = lax.rem(lax.div(me, NC), NZ)
    my_x = lax.div(me, NC * NZ)
    y_right = lax.rem(my_y + 1, NY)
    y_left = lax.rem(my_y + NY - 1, NY)
    y_far = lax.rem(my_y + 2, NY)

    def swap(m):
        return m if m == 0 or m == NZ - 1 else (m + 1 if m % 2 else m - 1)

    def shift_of(m, g):
        far = lax.div(m + 1, 2)
        odd = lax.rem(m + lax.div(g, near_group), 2)
        dz = odd * far + (1 - odd) * lax.rem(NZ - far, NZ)
        return lax.div(g, NC), dz, lax.rem(g, NC)

    def ahead(m, g):
        dx, dz, dc = shift_of(m, g)
        x, z, c = lax.rem(my_x + dx, NX), lax.rem(my_z + dz, NZ), lax.rem(my_c + dc, NC)
        return ((x * NZ + z) * NC + c, my_y)

    def behind(m, g):
        dx, dz, dc = shift_of(m, g)
        x, z, c = lax.rem(my_x + NX - dx, NX), lax.rem(my_z + NZ - dz, NZ), lax.rem(my_c + NC - dc, NC)
        return ((x * NZ + z) * NC + c, my_y)

    def plane(g):
        x, c = lax.rem(my_x + lax.div(g, NC), NX), lax.rem(my_c + lax.rem(g, NC), NC)
        return ((x * NZ + my_z) * NC + c, my_y)

    def plane_back(g):
        x, c = lax.rem(my_x + NX - lax.div(g, NC), NX), lax.rem(my_c + NC - lax.rem(g, NC), NC)
        return ((x * NZ + my_z) * NC + c, my_y)

    def push(src, dst, send_sem, recv_sem, to):
        pltpu.make_async_remote_copy(
            src_ref=src, dst_ref=dst, send_sem=send_sem, recv_sem=recv_sem,
            device_id=to, device_id_type=MESH,
        ).start()

    loads = [
        pltpu.make_async_copy(x_hbm, x_ref, load_sem.at[0]),
        pltpu.make_async_copy(ids_hbm, ids_ref, load_sem.at[1]),
        pltpu.make_async_copy(temp_hbm, temp_ref, load_sem.at[2]),
    ]
    for load in loads:
        load.start()

    barrier = pltpu.get_barrier_semaphore()

    @pl.loop(1, group)
    def _(g):
        pl.semaphore_signal(barrier, inc=1, device_id=plane(g), device_id_type=MESH)

    @pl.loop(1, NZ)
    def _(m):
        pl.semaphore_signal(barrier, inc=1, device_id=ahead(m, 0), device_id_type=MESH)

    for y in (y_right, y_left, y_far):
        pl.semaphore_signal(barrier, inc=1, device_id=(me, y), device_id_type=MESH)

    for load in loads:
        load.wait()
    x = x_ref[...]
    unit_rows = x * lax.rsqrt(jnp.sum(x * x, axis=1, keepdims=True) + 1e-06)
    unit[...] = unit_rows
    packed = unit_rows.astype(BF16)
    halves[:rows, :] = packed[:, :half]
    halves[rows:, :] = packed[:, half:]

    ids = ids_ref[...]
    owner = lax.div(ids, per_owner)
    dx = lax.rem(lax.div(owner, NC * NZ) - my_x + NX, NX)
    dz = lax.rem(lax.rem(lax.div(owner, NC), NZ) - my_z + NZ, NZ)
    dc = lax.rem(lax.rem(owner, NC) - my_c + NC, NC)
    g_of = dx * NC + dc
    up = jnp.where(g_of < near_group, 2 * dz - 1, 2 * dz)
    down = jnp.where(g_of < near_group, 2 * (NZ - dz), 2 * (NZ - dz) - 1)
    place = jnp.where(dz == 0, 0, jnp.where(dz == NZ // 2, NZ - 1, jnp.where(dz < NZ // 2, up, down)))
    offset = place * group + g_of
    offset_f = jnp.broadcast_to(offset.astype(F32), (rows, rows))
    same = offset_f == offset_f.T
    earlier = lax.broadcasted_iota(jnp.int32, (rows, rows), 0) < lax.broadcasted_iota(jnp.int32, (rows, rows), 1)
    rank = jnp.sum(jnp.where(same & earlier, 1.0, 0.0), axis=0, keepdims=True).astype(jnp.int32)
    target = offset * (2 * CAP) + rank
    targets = jnp.concatenate([target, target + CAP], axis=1)
    raw[0, 0, 0] = ids

    slab = group * 2 * CAP

    def pack(m):
        hit = lax.broadcasted_iota(jnp.int32, (slab, 2 * rows), 0) + m * slab == targets
        part = jnp.dot(jnp.where(hit, 1.0, 0.0).astype(BF16), halves[...], preferred_element_type=F32)
        send[m * group : (m + 1) * group] = part.astype(BF16).reshape(group, 2 * CAP, half)
        if m == 0:
            keys[0, 0] = send[0]

    def ship(m):
        @pl.loop(1 if m == 0 else 0, group)
        def _(g):
            k = m * group + g
            push(send.at[k], keys.at[0, k], row_send_sem, row_recv_sem.at[lax.div(g, near_group), m], ahead(m, g))

    pack(0)
    pl.semaphore_wait(barrier, group - 1 + NZ - 1 + NY - 1)

    @pl.loop(1, group)
    def _(g):
        pl.semaphore_signal(ready_sem, inc=1, device_id=plane(g), device_id_type=MESH)

    ship(0)
    for m in range(1, min(AHEAD, NZ)):
        pack(m)
    pl.semaphore_wait(ready_sem, group - 1)
    for m in range(1, min(AHEAD, NZ)):
        ship(m)

    @pl.loop(1, NZ)
    def _(m):
        push(raw.at[0, 0, 0], raw.at[0, m, 0], raw_send_sem.at[0], raw_z_sem, ahead(m, 0))

    def raw_plane():
        wait_bytes(raw.at[0, pl.ds(1, NZ - 1), 0], raw_z_sem)

        @pl.loop(1, group)
        def _(g):
            push(raw.at[0, :, 0], raw.at[0, :, g], raw_send_sem.at[1], raw_plane_sem, plane(g))

    def raw_y():
        wait_bytes(raw.at[0, :, pl.ds(1, group - 1)], raw_plane_sem)
        for n, (to, column) in enumerate(((y_right, 1), (y_left, 3), (y_far, 2))):
            push(raw.at[0], raw.at[column], raw_send_sem.at[2 + n], raw_y_sem.at[n], (me, to))

    def read_ids(column):
        parts = []
        for m in range(NZ):
            parts += [raw[column, m, :near_group], raw[column, swap(m), near_group:]]
        ids_of = jnp.broadcast_to(jnp.concatenate(parts, axis=0), (owners, CAP, rows)).reshape(slots, rows)
        mine = lax.div(ids_of, per_owner) == me
        below = (
            lax.broadcasted_iota(jnp.int32, (rows, rows), 0) < lax.broadcasted_iota(jnp.int32, (rows, rows), 1)
        )
        ranks = jnp.dot(
            jnp.where(mine, 1.0, 0.0).astype(BF16), jnp.where(below, 1.0, 0.0).astype(BF16),
            preferred_element_type=F32,
        )
        slot_rank = lax.rem(lax.broadcasted_iota(jnp.int32, (slots, rows), 0), CAP).astype(F32)
        value = (lax.rem(ids_of, per_owner) + 1).astype(F32)
        chosen = jnp.where(mine & (ranks == slot_rank), value, 0.0).astype(BF16)
        key_ids[column] = lax.dot_general(
            jnp.ones((8, rows), BF16), chosen, (((1,), (1,)), ((), ())), preferred_element_type=F32
        ) - 1.0
        return chosen

    strip = min(128, owners * 2 * CAP)
    targets_f = jnp.broadcast_to(targets.astype(F32), (strip, 2 * rows)).T
    lanes = lax.broadcasted_iota(jnp.int32, (2 * rows, strip), 1).astype(F32)
    for j in range(owners * 2 * CAP // strip):
        turned[:, j * strip : (j + 1) * strip] = jnp.where(lanes + j * strip == targets_f, 1.0, 0.0).astype(BF16)

    def unpack(column, m):
        part = keys[column, m * group : (m + 1) * group].astype(F32)
        first = column * slots + m * chunk_rows
        table[first : first + chunk_rows, :half] = part[:, :CAP, :].reshape(chunk_rows, half).astype(BF16)
        table[first : first + chunk_rows, half:] = part[:, CAP:, :].reshape(chunk_rows, half).astype(BF16)

    def chunk(column, m):
        return keys.at[column, pl.ds(m * group, group)]

    def part_of(column, m, part):
        return keys.at[column, pl.ds(m * group + part * near_group, near_group)]

    def relay(m):
        for way, to, column in ((0, y_right, 1), (1, y_left, 3)):
            wait_bytes(chunk(column, m), y_recv_sem.at[way, m])
            push(part_of(column, m, way), part_of(2, m, way), relay_send_sem.at[way], far_recv_sem.at[way, m], (me, to))
        unpack(1, m)
        unpack(3, m)

    block = min(256, slots)
    blocks = slots // block
    every = range(blocks - 1, -1, -1)
    best = [jnp.full((block, 1), LOWEST, F32) for _ in range(blocks)]
    query = []

    def read_all_ids():
        chosen = read_ids(0)
        query_id = jnp.dot(chosen, jnp.ones((rows, 128), BF16), preferred_element_type=F32)[:, 0:1] - 1.0
        query_temp = jnp.ones_like(query_id)
        for c in range(per_owner):
            query_temp = jnp.where(query_id == float(c), temp_ref[c], query_temp)
        query.append(jnp.where(query_id < 0.0, -2.0, query_id))
        query.append(query_temp)
        for n, column in enumerate((1, 3, 2)):
            wait_bytes(raw.at[column], raw_y_sem.at[n])
            read_ids(column)

    def score(column, first, count, which):
        query_id, query_temp = query
        base = column * slots + first
        for b in which:
            at = slice(b * block, (b + 1) * block)
            cosine = lax.dot_general(
                table[at, :], table[base : base + count, :], (((1,), (1,)), ((), ())),
                preferred_element_type=F32,
            )
            allowed = query_id[at] == key_ids[column, 0:1, first : first + count]
            if column == 0:
                allowed &= (
                    lax.broadcasted_iota(jnp.int32, (block, count), 0) + b * block
                    != lax.broadcasted_iota(jnp.int32, (block, count), 1) + first
                )
            scored = jnp.where(allowed, cosine * query_temp[at], LOWEST)
            scores[at, base : base + count] = scored
            best[b] = jnp.maximum(best[b], jnp.max(scored, axis=1, keepdims=True))

    def far(m):
        for way in range(2):
            wait_bytes(part_of(2, m, way), far_recv_sem.at[way, m])
        unpack(2, m)

    for m in range(NZ):
        for part in range(2):
            first = m * group + part * near_group
            mine = 1 if first == 0 else 0
            if near_group > mine:
                wait_bytes(keys.at[0, pl.ds(first + mine, near_group - mine)], row_recv_sem.at[part, m])
            push(part_of(0, m, part), part_of(1, m, part), y_send_sem.at[0], y_recv_sem.at[0, m], (me, y_right))
            push(part_of(0, m, part), part_of(3, m, part), y_send_sem.at[1], y_recv_sem.at[1, m], (me, y_left))
        if m + AHEAD < NZ:
            pack(m + AHEAD)
            ship(m + AHEAD)
        unpack(0, m)
        if m == min(1, NZ - 1):
            raw_plane()
        if m >= 1:
            relay(m - 1)
        if m == min(3, NZ - 1):
            raw_y()
        if m >= 2:
            far(m - 2)
        if m == min(5, NZ - 1):
            read_all_ids()
        if m == NZ - 1:
            score(0, 0, slots, every)
    relay(NZ - 1)
    score(1, 0, slots, every)
    score(3, 0, slots, every)
    half_slots = slots // 2
    late = range(max(NZ - 2, 0), NZ)
    for m in late:
        if m < NZ // 2:
            far(m)
    score(2, 0, half_slots, every)
    for m in late:
        if m >= NZ // 2:
            far(m)
    score(2, half_slots, half_slots, [blocks - 1])
    query_temp = query[1]

    per_block = block // CAP

    def similarities():
        for b in range(slots // block):
            close = best[b] / query_temp[b * block : (b + 1) * block]
            lane = lax.broadcasted_iota(jnp.int32, (block, 128), 1)
            rank_of = lax.rem(lax.broadcasted_iota(jnp.int32, (block, 128), 0), CAP)
            spread_close = jnp.sum(jnp.where(lane == rank_of, close, 0.0).reshape(per_block, CAP, 128), axis=1)
            for j in range(per_block):
                m, g = divmod(b * per_block + j, group)
                sim_send[m if g < near_group else swap(m), g] = spread_close[j : j + 1, :]
        sim_mid[0] = sim_send[0]

        @pl.loop(1, NZ)
        def _(m):
            push(sim_send.at[m], sim_mid.at[m], sim_send_sem.at[0], sim_z_sem, behind(m, 0))


    def way_back(m):
        @pl.loop(1 if m == 0 else 0, group)
        def _(g):
            k = m * group + g
            push(outs.at[k], back.at[k], back_send_sem, back_recv_sem.at[back_part(m)], behind(m, g))

    def back_part(m):
        return m * chunk_rows // fine

    fine = min(FINE, block)
    per_fine = fine // CAP
    parts = slots // fine
    for p in range(parts - 1, -1, -1):
        b, inner = divmod(p * fine, block)
        here = pl.ds(p * fine, fine)
        top = best[b][inner : inner + fine]
        total = jnp.zeros((fine, 1), F32)
        for column in range(NY):
            weight = jnp.exp(scores[here, column * slots : (column + 1) * slots] - top)
            total += jnp.sum(weight, axis=1, keepdims=True)
            weights[:fine, column * slots : (column + 1) * slots] = weight.astype(BF16)
        near = []
        for h in range(2):
            summed = jnp.dot(weights[:fine], table[:, h * half : (h + 1) * half], preferred_element_type=F32)
            near.append((summed / total).reshape(per_fine, CAP, half))
        outs[pl.ds(p * per_fine, per_fine)] = jnp.concatenate(near, axis=1).astype(BF16)
        if p == 0:
            back[0] = outs[0]
        if parts == 1:
            similarities()
        if p == max(parts // 2 - 1, 0):
            wait_bytes(sim_mid.at[pl.ds(1, NZ - 1)], sim_z_sem)
            sim_recv[:, 0] = sim_mid[:, 0]

            @pl.loop(1, group)
            def _(g):
                push(sim_mid.at[:, g], sim_recv.at[:, g], sim_send_sem.at[1], sim_plane_sem, plane_back(g))

        for n, m in enumerate(range((p + 1) * per_fine // group - 1, p * per_fine // group - 1, -1)):
            way_back(m)
            if p == parts - 1 and parts > 1 and n == 1:
                score(2, half_slots, half_slots, range(blocks - 2, -1, -1))
                similarities()

    others = pl.ds(1, owners - 1)
    wait_bytes(sim_recv.at[:, pl.ds(1, group - 1)], sim_plane_sem)
    got = []
    for k in range(owners):
        m, g = divmod(k, group)
        got.append(sim_recv[m if g < near_group else swap(m), g])
    at_offset = lax.broadcasted_iota(jnp.int32, (owners, rows), 0) == offset
    at_rank = lax.broadcasted_iota(jnp.int32, (128, rows), 0) == rank
    picked = lax.dot_general(
        jnp.concatenate(got, axis=0), jnp.where(at_offset, 1.0, 0.0), (((0,), (0,)), ((), ())),
        preferred_element_type=F32, precision=lax.Precision.HIGHEST,
    )
    sim_ref[...] = jnp.sum(jnp.where(at_rank, picked, 0.0), axis=0, keepdims=True)

    wait_bytes(send.at[others], row_send_sem)
    wait_bytes(sim_send.at[pl.ds(1, NZ - 1)], sim_send_sem.at[0])
    wait_bytes(sim_mid.at[:, pl.ds(1, group - 1)], sim_send_sem.at[1])
    wait_bytes(raw.at[0, pl.ds(1, NZ - 1), 0], raw_send_sem.at[0])
    wait_bytes(raw.at[0, :, pl.ds(1, group - 1)], raw_send_sem.at[1])
    for n in range(3):
        wait_bytes(raw.at[0], raw_send_sem.at[2 + n])
    for way in range(2):
        wait_bytes(keys.at[0], y_send_sem.at[way])
        wait_bytes(keys.at[0, pl.ds(0, owners // 2)], relay_send_sem.at[way])

    span = 2 * fine
    for p in range(parts - 1, -1, -1):
        first = max(p * per_fine, 1)
        wait_bytes(back.at[pl.ds(first, (p + 1) * per_fine - first)], back_recv_sem.at[p])
        returned = jnp.dot(
            turned[:, p * span : (p + 1) * span],
            back[p * per_fine : (p + 1) * per_fine].reshape(span, half),
            preferred_element_type=F32,
        )
        if p > 0:
            unit[:, :half] -= returned[:rows]
            unit[:, half:] -= returned[rows:]
        else:
            out_ref[:, :half] = unit[:, :half] - returned[:rows]
            out_ref[:, half:] = unit[:, half:] - returned[rows:]
    wait_bytes(outs.at[others], back_send_sem)


def per_device(embeds, cluster_ids, inv_temp):
    rows, width = embeds.shape
    group = NX * NC
    owners = group * NZ
    slots = owners * CAP
    half = width // 2
    block = min(256, slots)
    DMA = pltpu.SemaphoreType.DMA
    vmem = pl.BlockSpec(memory_space=pltpu.VMEM)
    hbm = pl.BlockSpec(memory_space=pltpu.HBM)
    residual, similarity = pl.pallas_call(
        kernel,
        out_shape=(jax.ShapeDtypeStruct((rows, width), F32), jax.ShapeDtypeStruct((1, rows), F32)),
        in_specs=[hbm, hbm, hbm],
        out_specs=(vmem, vmem),
        scratch_shapes=[
            pltpu.VMEM((1, rows), jnp.int32),
            pltpu.VMEM((rows, width), F32),
            pltpu.SMEM(inv_temp.shape, F32),
            pltpu.VMEM((rows, width), F32),
            pltpu.VMEM((2 * rows, half), BF16),
            pltpu.VMEM((owners, 2 * CAP, half), BF16),
            pltpu.VMEM((NY, owners, 2 * CAP, half), BF16),
            pltpu.VMEM((NY * slots, width), BF16),
            pltpu.VMEM((slots, NY * slots), F32),
            pltpu.VMEM((block, NY * slots), BF16),
            pltpu.VMEM((owners, 2 * CAP, half), BF16),
            pltpu.VMEM((owners, 2 * CAP, half), BF16),
            pltpu.VMEM((2 * rows, owners * 2 * CAP), BF16),
            pltpu.VMEM((NY, NZ, group, 1, rows), jnp.int32),
            pltpu.VMEM((NY, 8, slots), F32),
            pltpu.VMEM((NZ, group, 1, 128), F32),
            pltpu.VMEM((NZ, group, 1, 128), F32),
            pltpu.VMEM((NZ, group, 1, 128), F32),
            DMA((3,)), pltpu.SemaphoreType.REGULAR, DMA, DMA((2, NZ)), DMA((2,)), DMA((2,)),
            DMA((2, NZ)), DMA((2, NZ)), DMA((5,)), DMA, DMA, DMA((3,)),
            DMA, DMA((slots // min(FINE, slots),)), DMA((2,)), DMA, DMA,
        ],
        compiler_params=pltpu.CompilerParams(
            collective_id=0, has_side_effects=True, vmem_limit_bytes=48 * 1024 * 1024
        ),
    )(*(pltpu.with_memory_space_constraint(a, pltpu.HBM) for a in (cluster_ids.reshape(1, rows), embeds, inv_temp)))
    return residual, similarity.reshape(rows)


def solution(mesh):
    in_specs = (P(("dp", "clus"), None), P(("dp", "clus")), P("dp"))
    out_specs = (P(("dp", "clus"), None), P(("dp", "clus")))
    return jax.shard_map(
        per_device, mesh=mesh, in_specs=in_specs, out_specs=out_specs, check_vma=False
    )
```

```python
import functools

import jax
import jax.numpy as jnp
from jax import lax
from jax.experimental import pallas as pl
from jax.experimental.pallas import tpu as pltpu
from jax.sharding import PartitionSpec as P

NX, NZ, NC, NY = 4, 8, 2, 4
CAP = 8
LOWEST = -1e30
FINE = 128
AHEAD = 3
MESH = pl.DeviceIdType.MESH
F32 = jnp.float32
BF16 = jnp.bfloat16


def wait_bytes(ref, sem):
    pltpu.make_async_copy(ref, ref, sem).wait()


def kernel(
    ids_hbm, x_hbm, temp_hbm, out_ref, sim_ref,
    ids_ref, x_ref, temp_ref, unit, halves, send, keys, table, scores, weights, outs, back, turned,
    raw, key_ids, sim_send, sim_mid, sim_recv,
    load_sem, ready_sem, row_send_sem, row_recv_sem, y_send_sem, relay_send_sem,
    y_recv_sem, far_recv_sem, raw_send_sem, raw_z_sem, raw_plane_sem, raw_y_sem,
    back_send_sem, back_recv_sem, sim_send_sem, sim_z_sem, sim_plane_sem,
):
    group = NX * NC
    owners = group * NZ
    rows, width = x_ref.shape
    half = width // 2
    slots = owners * CAP
    per_owner = temp_ref.shape[0]
    chunk_rows = group * CAP
    near_group = group // 2

    me = lax.axis_index("dp")
    my_y = lax.axis_index("clus")
    my_c = lax.rem(me, NC)
    my_z = lax.rem(lax.div(me, NC), NZ)
    my_x = lax.div(me, NC * NZ)
    y_right = lax.rem(my_y + 1, NY)
    y_left = lax.rem(my_y + NY - 1, NY)
    y_far = lax.rem(my_y + 2, NY)

    def swap(m):
        return m if m == 0 or m == NZ - 1 else (m + 1 if m % 2 else m - 1)

    def shift_of(m, g):
        far = lax.div(m + 1, 2)
        odd = lax.rem(m + lax.div(g, near_group), 2)
        dz = odd * far + (1 - odd) * lax.rem(NZ - far, NZ)
        return lax.div(g, NC), dz, lax.rem(g, NC)

    def ahead(m, g):
        dx, dz, dc = shift_of(m, g)
        x, z, c = lax.rem(my_x + dx, NX), lax.rem(my_z + dz, NZ), lax.rem(my_c + dc, NC)
        return ((x * NZ + z) * NC + c, my_y)

    def behind(m, g):
        dx, dz, dc = shift_of(m, g)
        x, z, c = lax.rem(my_x + NX - dx, NX), lax.rem(my_z + NZ - dz, NZ), lax.rem(my_c + NC - dc, NC)
        return ((x * NZ + z) * NC + c, my_y)

    def plane(g):
        x, c = lax.rem(my_x + lax.div(g, NC), NX), lax.rem(my_c + lax.rem(g, NC), NC)
        return ((x * NZ + my_z) * NC + c, my_y)

    def plane_back(g):
        x, c = lax.rem(my_x + NX - lax.div(g, NC), NX), lax.rem(my_c + NC - lax.rem(g, NC), NC)
        return ((x * NZ + my_z) * NC + c, my_y)

    def push(src, dst, send_sem, recv_sem, to):
        pltpu.make_async_remote_copy(
            src_ref=src, dst_ref=dst, send_sem=send_sem, recv_sem=recv_sem,
            device_id=to, device_id_type=MESH,
        ).start()

    loads = [
        pltpu.make_async_copy(x_hbm, x_ref, load_sem.at[0]),
        pltpu.make_async_copy(ids_hbm, ids_ref, load_sem.at[1]),
        pltpu.make_async_copy(temp_hbm, temp_ref, load_sem.at[2]),
    ]
    for load in loads:
        load.start()

    barrier = pltpu.get_barrier_semaphore()

    @pl.loop(1, group)
    def _(g):
        pl.semaphore_signal(barrier, inc=1, device_id=plane(g), device_id_type=MESH)

    @pl.loop(1, NZ)
    def _(m):
        pl.semaphore_signal(barrier, inc=1, device_id=ahead(m, 0), device_id_type=MESH)

    for y in (y_right, y_left, y_far):
        pl.semaphore_signal(barrier, inc=1, device_id=(me, y), device_id_type=MESH)

    for load in loads:
        load.wait()
    x = x_ref[...]
    unit_rows = x * lax.rsqrt(jnp.sum(x * x, axis=1, keepdims=True) + 1e-06)
    unit[...] = unit_rows
    packed = unit_rows.astype(BF16)
    halves[:rows, :] = packed[:, :half]
    halves[rows:, :] = packed[:, half:]

    ids = ids_ref[...]
    owner = lax.div(ids, per_owner)
    dx = lax.rem(lax.div(owner, NC * NZ) - my_x + NX, NX)
    dz = lax.rem(lax.rem(lax.div(owner, NC), NZ) - my_z + NZ, NZ)
    dc = lax.rem(lax.rem(owner, NC) - my_c + NC, NC)
    g_of = dx * NC + dc
    up = jnp.where(g_of < near_group, 2 * dz - 1, 2 * dz)
    down = jnp.where(g_of < near_group, 2 * (NZ - dz), 2 * (NZ - dz) - 1)
    place = jnp.where(dz == 0, 0, jnp.where(dz == NZ // 2, NZ - 1, jnp.where(dz < NZ // 2, up, down)))
    offset = place * group + g_of
    offset_f = jnp.broadcast_to(offset.astype(F32), (rows, rows))
    same = offset_f == offset_f.T
    earlier = lax.broadcasted_iota(jnp.int32, (rows, rows), 0) < lax.broadcasted_iota(jnp.int32, (rows, rows), 1)
    rank = jnp.sum(jnp.where(same & earlier, 1.0, 0.0), axis=0, keepdims=True).astype(jnp.int32)
    target = offset * (2 * CAP) + rank
    targets = jnp.concatenate([target, target + CAP], axis=1)
    raw[0, 0, 0] = ids

    slab = group * 2 * CAP

    def pack(m):
        hit = lax.broadcasted_iota(jnp.int32, (slab, 2 * rows), 0) + m * slab == targets
        part = jnp.dot(jnp.where(hit, 1.0, 0.0).astype(BF16), halves[...], preferred_element_type=F32)
        send[m * group : (m + 1) * group] = part.astype(BF16).reshape(group, 2 * CAP, half)
        if m == 0:
            keys[0, 0] = send[0]

    def ship(m):
        @pl.loop(1 if m == 0 else 0, group)
        def _(g):
            k = m * group + g
            push(send.at[k], keys.at[0, k], row_send_sem, row_recv_sem.at[lax.div(g, near_group), m], ahead(m, g))

    pack(0)
    pl.semaphore_wait(barrier, group - 1 + NZ - 1 + NY - 1)

    @pl.loop(1, group)
    def _(g):
        pl.semaphore_signal(ready_sem, inc=1, device_id=plane(g), device_id_type=MESH)

    ship(0)
    for m in range(1, min(AHEAD, NZ)):
        pack(m)
    pl.semaphore_wait(ready_sem, group - 1)
    for m in range(1, min(AHEAD, NZ)):
        ship(m)

    @pl.loop(1, NZ)
    def _(m):
        push(raw.at[0, 0, 0], raw.at[0, m, 0], raw_send_sem.at[0], raw_z_sem, ahead(m, 0))

    def raw_plane():
        wait_bytes(raw.at[0, pl.ds(1, NZ - 1), 0], raw_z_sem)

        @pl.loop(1, group)
        def _(g):
            push(raw.at[0, :, 0], raw.at[0, :, g], raw_send_sem.at[1], raw_plane_sem, plane(g))

    def raw_y():
        wait_bytes(raw.at[0, :, pl.ds(1, group - 1)], raw_plane_sem)
        read_query_ids()
        for n, (to, column) in enumerate(((y_right, 1), (y_left, 3), (y_far, 2))):
            push(key_ids.at[0], key_ids.at[column], raw_send_sem.at[2 + n], raw_y_sem.at[n], (me, to))

    def read_ids(column):
        parts = []
        for m in range(NZ):
            parts += [raw[column, m, :near_group], raw[column, swap(m), near_group:]]
        ids_of = jnp.broadcast_to(jnp.concatenate(parts, axis=0), (owners, CAP, rows)).reshape(slots, rows)
        mine = lax.div(ids_of, per_owner) == me
        below = (
            lax.broadcasted_iota(jnp.int32, (rows, rows), 0) < lax.broadcasted_iota(jnp.int32, (rows, rows), 1)
        )
        ranks = jnp.dot(
            jnp.where(mine, 1.0, 0.0).astype(BF16), jnp.where(below, 1.0, 0.0).astype(BF16),
            preferred_element_type=F32,
        )
        slot_rank = lax.rem(lax.broadcasted_iota(jnp.int32, (slots, rows), 0), CAP).astype(F32)
        value = (lax.rem(ids_of, per_owner) + 1).astype(F32)
        chosen = jnp.where(mine & (ranks == slot_rank), value, 0.0).astype(BF16)
        key_ids[column] = lax.dot_general(
            jnp.ones((8, rows), BF16), chosen, (((1,), (1,)), ((), ())), preferred_element_type=F32
        )[0:1] - 1.0
        return chosen

    strip = min(128, owners * 2 * CAP)
    targets_f = jnp.broadcast_to(targets.astype(F32), (strip, 2 * rows)).T
    lanes = lax.broadcasted_iota(jnp.int32, (2 * rows, strip), 1).astype(F32)
    for j in range(owners * 2 * CAP // strip):
        turned[:, j * strip : (j + 1) * strip] = jnp.where(lanes + j * strip == targets_f, 1.0, 0.0).astype(BF16)

    def unpack(column, m):
        part = keys[column, m * group : (m + 1) * group].astype(F32)
        first = column * slots + m * chunk_rows
        table[first : first + chunk_rows, :half] = part[:, :CAP, :].reshape(chunk_rows, half).astype(BF16)
        table[first : first + chunk_rows, half:] = part[:, CAP:, :].reshape(chunk_rows, half).astype(BF16)

    def chunk(column, m):
        return keys.at[column, pl.ds(m * group, group)]

    def part_of(column, m, part):
        return keys.at[column, pl.ds(m * group + part * near_group, near_group)]

    def relay(m):
        for way, to, column in ((0, y_right, 1), (1, y_left, 3)):
            wait_bytes(chunk(column, m), y_recv_sem.at[way, m])
            push(part_of(column, m, way), part_of(2, m, way), relay_send_sem.at[way], far_recv_sem.at[way, m], (me, to))
        unpack(1, m)
        unpack(3, m)

    block = min(256, slots)
    blocks = slots // block
    every = range(blocks - 1, -1, -1)
    best = [jnp.full((block, 1), LOWEST, F32) for _ in range(blocks)]
    query = []

    def read_query_ids():
        chosen = read_ids(0)
        query_id = jnp.dot(chosen, jnp.ones((rows, 128), BF16), preferred_element_type=F32)[:, 0:1] - 1.0
        query_temp = jnp.ones_like(query_id)
        for c in range(per_owner):
            query_temp = jnp.where(query_id == float(c), temp_ref[c], query_temp)
        query.append(jnp.where(query_id < 0.0, -2.0, query_id))
        query.append(query_temp)

    def wait_ids():
        for n, column in enumerate((1, 3, 2)):
            wait_bytes(key_ids.at[column], raw_y_sem.at[n])

    def score(column, first, count, which):
        query_id, query_temp = query
        base = column * slots + first
        for b in which:
            at = slice(b * block, (b + 1) * block)
            cosine = lax.dot_general(
                table[at, :], table[base : base + count, :], (((1,), (1,)), ((), ())),
                preferred_element_type=F32,
            )
            allowed = query_id[at] == key_ids[column, 0:1, first : first + count]
            if column == 0:
                allowed &= (
                    lax.broadcasted_iota(jnp.int32, (block, count), 0) + b * block
                    != lax.broadcasted_iota(jnp.int32, (block, count), 1) + first
                )
            scored = jnp.where(allowed, cosine * query_temp[at], LOWEST)
            scores[at, base : base + count] = scored
            best[b] = jnp.maximum(best[b], jnp.max(scored, axis=1, keepdims=True))

    def far(m):
        for way in range(2):
            wait_bytes(part_of(2, m, way), far_recv_sem.at[way, m])
        unpack(2, m)

    for m in range(NZ):
        for part in range(2):
            first = m * group + part * near_group
            mine = 1 if first == 0 else 0
            if near_group > mine:
                wait_bytes(keys.at[0, pl.ds(first + mine, near_group - mine)], row_recv_sem.at[part, m])
            push(part_of(0, m, part), part_of(1, m, part), y_send_sem.at[0], y_recv_sem.at[0, m], (me, y_right))
            push(part_of(0, m, part), part_of(3, m, part), y_send_sem.at[1], y_recv_sem.at[1, m], (me, y_left))
        if m + AHEAD < NZ:
            pack(m + AHEAD)
            ship(m + AHEAD)
        unpack(0, m)
        if m == min(1, NZ - 1):
            raw_plane()
        if m >= 1:
            relay(m - 1)
        if m == min(3, NZ - 1):
            raw_y()
        if m >= 2:
            far(m - 2)
        if m == min(5, NZ - 1):
            wait_ids()
        if m == NZ - 1:
            score(0, 0, slots, every)
    relay(NZ - 1)
    score(1, 0, slots, every)
    score(3, 0, slots, every)
    half_slots = slots // 2
    late = range(max(NZ - 2, 0), NZ)
    for m in late:
        if m < NZ // 2:
            far(m)
    score(2, 0, half_slots, every)
    for m in late:
        if m >= NZ // 2:
            far(m)
    score(2, half_slots, half_slots, [blocks - 1])
    query_temp = query[1]

    per_block = block // CAP

    def similarities():
        for b in range(slots // block):
            close = best[b] / query_temp[b * block : (b + 1) * block]
            lane = lax.broadcasted_iota(jnp.int32, (block, 128), 1)
            rank_of = lax.rem(lax.broadcasted_iota(jnp.int32, (block, 128), 0), CAP)
            spread_close = jnp.sum(jnp.where(lane == rank_of, close, 0.0).reshape(per_block, CAP, 128), axis=1)
            for j in range(per_block):
                m, g = divmod(b * per_block + j, group)
                sim_send[m if g < near_group else swap(m), g] = spread_close[j : j + 1, :]
        sim_mid[0] = sim_send[0]

        @pl.loop(1, NZ)
        def _(m):
            push(sim_send.at[m], sim_mid.at[m], sim_send_sem.at[0], sim_z_sem, behind(m, 0))


    def way_back(m):
        @pl.loop(1 if m == 0 else 0, group)
        def _(g):
            k = m * group + g
            push(outs.at[k], back.at[k], back_send_sem, back_recv_sem.at[back_part(m)], behind(m, g))

    def back_part(m):
        return m * chunk_rows // fine

    fine = min(FINE, block)
    per_fine = fine // CAP
    parts = slots // fine
    for p in range(parts - 1, -1, -1):
        b, inner = divmod(p * fine, block)
        here = pl.ds(p * fine, fine)
        top = best[b][inner : inner + fine]
        total = jnp.zeros((fine, 1), F32)
        for column in range(NY):
            weight = jnp.exp(scores[here, column * slots : (column + 1) * slots] - top)
            total += jnp.sum(weight, axis=1, keepdims=True)
            weights[:fine, column * slots : (column + 1) * slots] = weight.astype(BF16)
        near = []
        for h in range(2):
            summed = jnp.dot(weights[:fine], table[:, h * half : (h + 1) * half], preferred_element_type=F32)
            near.append((summed / total).reshape(per_fine, CAP, half))
        outs[pl.ds(p * per_fine, per_fine)] = jnp.concatenate(near, axis=1).astype(BF16)
        if p == 0:
            back[0] = outs[0]
        if parts == 1:
            similarities()
        if p == max(parts // 2 - 1, 0):
            wait_bytes(sim_mid.at[pl.ds(1, NZ - 1)], sim_z_sem)
            sim_recv[:, 0] = sim_mid[:, 0]

            @pl.loop(1, group)
            def _(g):
                push(sim_mid.at[:, g], sim_recv.at[:, g], sim_send_sem.at[1], sim_plane_sem, plane_back(g))

        for n, m in enumerate(range((p + 1) * per_fine // group - 1, p * per_fine // group - 1, -1)):
            way_back(m)
            if p == parts - 1 and parts > 1 and n == 1:
                score(2, half_slots, half_slots, range(blocks - 2, -1, -1))
                similarities()

    others = pl.ds(1, owners - 1)
    wait_bytes(sim_recv.at[:, pl.ds(1, group - 1)], sim_plane_sem)
    got = []
    for k in range(owners):
        m, g = divmod(k, group)
        got.append(sim_recv[m if g < near_group else swap(m), g])
    at_offset = lax.broadcasted_iota(jnp.int32, (owners, rows), 0) == offset
    at_rank = lax.broadcasted_iota(jnp.int32, (128, rows), 0) == rank
    picked = lax.dot_general(
        jnp.concatenate(got, axis=0), jnp.where(at_offset, 1.0, 0.0), (((0,), (0,)), ((), ())),
        preferred_element_type=F32, precision=lax.Precision.HIGHEST,
    )
    sim_ref[...] = jnp.sum(jnp.where(at_rank, picked, 0.0), axis=0, keepdims=True)

    wait_bytes(send.at[others], row_send_sem)
    wait_bytes(sim_send.at[pl.ds(1, NZ - 1)], sim_send_sem.at[0])
    wait_bytes(sim_mid.at[:, pl.ds(1, group - 1)], sim_send_sem.at[1])
    wait_bytes(raw.at[0, pl.ds(1, NZ - 1), 0], raw_send_sem.at[0])
    wait_bytes(raw.at[0, :, pl.ds(1, group - 1)], raw_send_sem.at[1])
    for n in range(3):
        wait_bytes(key_ids.at[0], raw_send_sem.at[2 + n])
    for way in range(2):
        wait_bytes(keys.at[0], y_send_sem.at[way])
        wait_bytes(keys.at[0, pl.ds(0, owners // 2)], relay_send_sem.at[way])

    span = 2 * fine
    for p in range(parts - 1, -1, -1):
        first = max(p * per_fine, 1)
        wait_bytes(back.at[pl.ds(first, (p + 1) * per_fine - first)], back_recv_sem.at[p])
        returned = jnp.dot(
            turned[:, p * span : (p + 1) * span],
            back[p * per_fine : (p + 1) * per_fine].reshape(span, half),
            preferred_element_type=F32,
        )
        if p > 0:
            unit[:, :half] -= returned[:rows]
            unit[:, half:] -= returned[rows:]
        else:
            out_ref[:, :half] = unit[:, :half] - returned[:rows]
            out_ref[:, half:] = unit[:, half:] - returned[rows:]
    wait_bytes(outs.at[others], back_send_sem)


def per_device(embeds, cluster_ids, inv_temp):
    rows, width = embeds.shape
    group = NX * NC
    owners = group * NZ
    slots = owners * CAP
    half = width // 2
    block = min(256, slots)
    DMA = pltpu.SemaphoreType.DMA
    vmem = pl.BlockSpec(memory_space=pltpu.VMEM)
    hbm = pl.BlockSpec(memory_space=pltpu.HBM)
    residual, similarity = pl.pallas_call(
        kernel,
        out_shape=(jax.ShapeDtypeStruct((rows, width), F32), jax.ShapeDtypeStruct((1, rows), F32)),
        in_specs=[hbm, hbm, hbm],
        out_specs=(vmem, vmem),
        scratch_shapes=[
            pltpu.VMEM((1, rows), jnp.int32),
            pltpu.VMEM((rows, width), F32),
            pltpu.SMEM(inv_temp.shape, F32),
            pltpu.VMEM((rows, width), F32),
            pltpu.VMEM((2 * rows, half), BF16),
            pltpu.VMEM((owners, 2 * CAP, half), BF16),
            pltpu.VMEM((NY, owners, 2 * CAP, half), BF16),
            pltpu.VMEM((NY * slots, width), BF16),
            pltpu.VMEM((slots, NY * slots), F32),
            pltpu.VMEM((block, NY * slots), BF16),
            pltpu.VMEM((owners, 2 * CAP, half), BF16),
            pltpu.VMEM((owners, 2 * CAP, half), BF16),
            pltpu.VMEM((2 * rows, owners * 2 * CAP), BF16),
            pltpu.VMEM((1, NZ, group, 1, rows), jnp.int32),
            pltpu.VMEM((NY, 1, slots), F32),
            pltpu.VMEM((NZ, group, 1, 128), F32),
            pltpu.VMEM((NZ, group, 1, 128), F32),
            pltpu.VMEM((NZ, group, 1, 128), F32),
            DMA((3,)), pltpu.SemaphoreType.REGULAR, DMA, DMA((2, NZ)), DMA((2,)), DMA((2,)),
            DMA((2, NZ)), DMA((2, NZ)), DMA((5,)), DMA, DMA, DMA((3,)),
            DMA, DMA((slots // min(FINE, slots),)), DMA((2,)), DMA, DMA,
        ],
        compiler_params=pltpu.CompilerParams(
            collective_id=0, has_side_effects=True, vmem_limit_bytes=48 * 1024 * 1024
        ),
    )(*(pltpu.with_memory_space_constraint(a, pltpu.HBM) for a in (cluster_ids.reshape(1, rows), embeds, inv_temp)))
    return residual, similarity.reshape(rows)


def solution(mesh):
    in_specs = (P(("dp", "clus"), None), P(("dp", "clus")), P("dp"))
    out_specs = (P(("dp", "clus"), None), P(("dp", "clus")))
    return jax.shard_map(
        per_device, mesh=mesh, in_specs=in_specs, out_specs=out_specs, check_vma=False
    )
```
